32 devices in a mesh: seq: 8 (over z, x), ch: 4 (over y, core).
Axes of the slice: x: 2, y: 2, z: 4, core: 2. Of those that a mesh axis runs over, the one named last changes fastest.
Arguments:
- value_proj: bfloat16 [3072, 512], P('seq', 'ch'), may hold values from -6 to 6
- gate_in: bfloat16 [3072, 512], P('seq', 'ch'), may hold values from -6 to 6
- gate_out: bfloat16 [3072, 512], P('seq', 'ch'), may hold values from -6 to 6
- skip_gain: float32 [512], P('ch'), may hold values from -3 to 3
- filter_taps: float32 [1536], replicated, may hold values from -0.15625 to 0.15625
- doc_lengths: int32 [3], replicated, may hold values from 1 to 4, 8 in all
- cotangent: bfloat16 [3072, 512], P('seq', 'ch'), may hold values from -6 to 6
Outputs:
- layer_out: bfloat16 [3072, 512], P('seq', 'ch')
- grad_value: bfloat16 [3072, 512], P('seq', 'ch')
- grad_gate: bfloat16 [3072, 512], P('seq', 'ch')
- filter_grad: float32 [1536], P('seq')
The draws below stay inside these ranges and needn't reach their ends.
Inputs may be any that keep to these rules, and one draw needn't show every extreme that they name: doc_lengths lists, in order, the lengths in shards of 384 tokens of the 3 documents that fill the sequence; they add up to the number of shards, and the longest is exactly 4.
All inputs are finite; a program needn't handle non-finite values.
Results may differ from the reference program's by a relative error of at most 0.0055.
Values may be sent and summed in bfloat16 or wider, within the bound.
No kernel may reach another device: no remote copies, remote signals or barrier semaphores. Data moves between devices by JAX's collectives and lax.ppermute only.
A program may use at most 64 MiB of HBM per device.

```python
import math
import jax
import jax.numpy as jnp
import numpy as np
from jax import lax

TOK_DEV = 384
GROUP_CH = 512
MOST = 4
DOCS = 3
MAXLAG = 1536
TOKENS = 3072
N_SEQ = 8


def shard_levels(key, dims, shards, low, largest):
    gain = 1.0
    for axis_at, shards_of in shards:
        steps = jax.random.uniform(jax.random.fold_in(jax.random.fold_in(key, 6), axis_at), (shards_of,), jnp.float32, low / len(shards), largest / len(shards))
        gain = gain * jnp.repeat(jnp.exp(steps), dims[axis_at] // shards_of).reshape((-1,) + (1,) * (len(dims) - 1 - axis_at))
    return gain


def length_profile(number_of, total, bound, lean):
    loads = [(1 << 20) // math.isqrt(rank ** lean) + 1 for rank in range(2, number_of + 1)]
    spare, counts = total - bound - (number_of - 1), [1] * (number_of - 1)
    while spare > 0:
        movable = [i for i in range(number_of - 1) if counts[i] < bound]
        whole, left = sum([loads[i] for i in movable]), spare
        for i in movable:
            addition = min(bound - counts[i], max(1, left * loads[i] // whole), spare)
            counts[i] = counts[i] + addition
            spare = spare - addition
    return np.array([bound] + counts)


def ragged_sizes(key, amount, total, bound, skew):
    if amount == 2:
        one = jax.random.randint(key, (), max(1, total - bound), min(bound, total - 1) + 1)
        return jnp.stack([one, total - one])
    tallies = jnp.asarray(length_profile(amount, total, bound, skew), jnp.int32)
    twos = (amount - 1) // 2
    source_of, taker = tallies[1:1 + 2 * twos:2], tallies[2:2 + 2 * twos:2]
    slack = jnp.minimum(source_of - 1, bound - taker)
    moved = jax.random.randint(jax.random.fold_in(key, 1), (twos,), 0, 1 << 20) % (slack + 1)
    tallies = tallies.at[1:1 + 2 * twos:2].set(source_of - moved).at[2:2 + 2 * twos:2].set(taker + moved)
    return tallies[jax.random.permutation(jax.random.fold_in(key, 2), amount)]


def bell_draw(key, dims, scale, most, split=(), held_as=jnp.bfloat16):
    entries = jax.random.normal(key, dims, jnp.float32) * scale
    if len(split) > 0:
        entries = shard_levels(key, dims, split, -0.22, 0.18) * entries
    return jnp.clip(entries, min=-most, max=most).astype(held_as)


def setup_inputs(seed: int = 0) -> dict:
    seeds = jax.random.split(jax.random.key(seed), 8)
    value_proj = bell_draw(seeds[0], (TOKENS, GROUP_CH), 1.0, 6.0, ((0, 8), (1, 4)))
    gate_in = bell_draw(seeds[1], (TOKENS, GROUP_CH), 1.0, 6.0, ((0, 8), (1, 4)))
    gate_out = bell_draw(seeds[2], (TOKENS, GROUP_CH), 1.0, 6.0, ((0, 8), (1, 4)))
    skip_gain = bell_draw(seeds[3], (GROUP_CH,), 0.5, 3.0, ((0, 4),), jnp.float32)
    filter_taps = bell_draw(seeds[4], (MAXLAG,), MAXLAG ** -0.5, 0.15625, (), jnp.float32)
    doc_lengths = ragged_sizes(seeds[5], DOCS, N_SEQ, MOST, 1).astype(jnp.int32)
    cotangent = bell_draw(seeds[6], (TOKENS, GROUP_CH), 1.0, 6.0, ((0, 8), (1, 4)))
    return dict(value_proj=value_proj, gate_in=gate_in, gate_out=gate_out, skip_gain=skip_gain, filter_taps=filter_taps, doc_lengths=doc_lengths, cotangent=cotangent)


def channel_part(gated_part, cot_part, padded_taps, doc_start, doc_end):
    blocks_count, block_rows, chans_part = gated_part.shape
    width = 2 * block_rows
    block_index = jnp.arange(blocks_count, dtype=jnp.int32)
    gated_freq = jnp.fft.rfft(gated_part, n=width, axis=1)
    cot_freq = jnp.fft.rfft(cot_part, n=width, axis=1)
    convolved = jnp.zeros(gated_part.shape, jnp.float32)
    transposed = jnp.zeros(gated_part.shape, jnp.float32)
    lag_sums = jnp.zeros(padded_taps.shape, jnp.float32)
    for offset in range(MOST):
        base_lag = offset * block_rows
        wrapped = jnp.concatenate([padded_taps[base_lag + block_rows:base_lag + 2 * block_rows], padded_taps[base_lag:base_lag + block_rows]])
        taps_freq = jnp.fft.rfft(wrapped)
        forward_ok = (block_index - offset >= doc_start)[:, None, None]
        shifted = jnp.roll(gated_freq, offset, axis=0)
        partial_fwd = jnp.fft.irfft(shifted * taps_freq[None, :, None], n=width, axis=1)[:, :block_rows]
        convolved = convolved + jnp.where(forward_ok, partial_fwd, 0.0)
        cross_spec = lax.optimization_barrier(jnp.sum(jnp.where(forward_ok, cot_freq * jnp.conj(shifted), 0.0), axis=(0, 2)))
        circular = jnp.fft.irfft(cross_spec, n=width)
        diag_sums = jnp.concatenate([circular[block_rows + 1:], circular[:block_rows]])
        lag_sums = lag_sums.at[base_lag + 1:base_lag + width].add(diag_sums)
        backward_ok = (block_index + offset < doc_end)[:, None, None]
        pulled = jnp.roll(cot_freq, -offset, axis=0)
        partial_bwd = jnp.fft.irfft(pulled * jnp.conj(taps_freq)[None, :, None], n=width, axis=1)[:, :block_rows]
        transposed = transposed + jnp.where(backward_ok, partial_bwd, 0.0)
    return (convolved, transposed, lag_sums)

def reference(value_proj, gate_in, gate_out, skip_gain, filter_taps, doc_lengths, cotangent):
    blocks_count = TOKENS // TOK_DEV
    gated = lax.optimization_barrier((gate_in.astype(jnp.float32) * value_proj.astype(jnp.float32)).astype(jnp.bfloat16)).astype(jnp.float32)
    cot_gated = lax.optimization_barrier((cotangent.astype(jnp.float32) * gate_out.astype(jnp.float32)).astype(jnp.bfloat16)).astype(jnp.float32)
    rounded_taps = lax.optimization_barrier(filter_taps.astype(jnp.bfloat16)).astype(jnp.float32)
    zero_rim = jnp.zeros((TOK_DEV,), jnp.float32)
    padded_taps = jnp.concatenate([zero_rim, rounded_taps, zero_rim])
    doc_ends = jnp.cumsum(doc_lengths)
    block_index = jnp.arange(blocks_count, dtype=jnp.int32)
    passed = doc_ends[None, :] <= block_index[:, None]
    doc_start = lax.optimization_barrier(jnp.sum(jnp.where(passed, doc_lengths[None, :], 0), axis=1))
    doc_end = lax.optimization_barrier(jnp.min(jnp.where(passed, doc_ends[-1], doc_ends[None, :]), axis=1))
    gated_blocks = gated.reshape(blocks_count, TOK_DEV, GROUP_CH)
    cot_blocks = cot_gated.reshape(blocks_count, TOK_DEV, GROUP_CH)
    pieces = max(1, GROUP_CH // 128)
    per_piece = GROUP_CH // pieces
    conv_parts = []
    back_parts = []
    lag_total = jnp.zeros(padded_taps.shape, jnp.float32)
    for piece_index in range(pieces):
        first_col = piece_index * per_piece
        conv_piece, back_piece, lag_piece = channel_part(gated_blocks[:, :, first_col:first_col + per_piece], cot_blocks[:, :, first_col:first_col + per_piece], padded_taps, doc_start, doc_end)
        conv_parts.append(conv_piece)
        back_parts.append(back_piece)
        lag_total = lag_total + lag_piece
    convolved = jnp.concatenate(conv_parts, axis=2).reshape(TOKENS, GROUP_CH)
    transposed = jnp.concatenate(back_parts, axis=2).reshape(TOKENS, GROUP_CH)
    skip_row = skip_gain[None, :]
    layer_out = (gate_out.astype(jnp.float32) * (convolved + skip_row * gated)).astype(jnp.bfloat16)
    through = transposed + skip_row * cot_gated
    grad_value = (through * gate_in.astype(jnp.float32)).astype(jnp.bfloat16)
    grad_gate = (through * value_proj.astype(jnp.float32)).astype(jnp.bfloat16)
    grad_scale = 1.0 / math.sqrt(TOKENS * GROUP_CH)
    filter_grad = lag_total[TOK_DEV:TOK_DEV + MAXLAG] * grad_scale
    return (layer_out, grad_value, grad_gate, filter_grad)
```

```python
import functools
import math

import jax
import jax.numpy as jnp
from jax import lax
from jax.experimental import pallas as pl
from jax.experimental.pallas import tpu as pltpu
from jax.sharding import PartitionSpec as P

TILE = 128
LIMIT = 8 * 1024 * 1024
LAGF = 10**10
CONVF = 10**10
F32 = jnp.float32
BF16 = jnp.bfloat16


def shifted(value, axis, by):
    length = lax.axis_size(axis)
    pairs = [(i, i + by) for i in range(length) if 0 <= i + by < length]
    return lax.ppermute(value, axis, pairs)


def doc_bounds(lengths_ref, position):
    start, stop, end = 0, 0, 0
    for k in range(lengths_ref.shape[0]):
        begin, end = end, end + lengths_ref[k]
        inside = jnp.logical_and(begin <= position, position < end)
        start = jnp.where(inside, begin, start)
        stop = jnp.where(inside, end, stop)
    return start, stop


def flip_matrix():
    row = lax.broadcasted_iota(jnp.int32, (TILE, TILE), 0)
    col = lax.broadcasted_iota(jnp.int32, (TILE, TILE), 1)
    return (row + col == TILE - 1).astype(F32).astype(BF16)


def masks_kernel(lengths_ref, gate_out_ref, skip_ref, masks_ref, gate_ref, skip_out_ref):
    longest = masks_ref.shape[0] // 2
    gate_ref[...] = gate_out_ref[...]
    skip_out_ref[...] = skip_ref[...]
    position = lax.axis_index("seq")
    start, stop = doc_bounds(lengths_ref, position)
    for k in range(longest):
        for n, ok in ((k, position - k >= start), (longest + k, position + k < stop)):
            masks_ref[n] = jnp.full(masks_ref.shape[1:], ok.astype(F32)).astype(BF16)


def lag_kernel(masks_ref, flipped_ref, before_ref, cots_ref, parts_ref, sources_ref, *, owned, copies, scale):
    evens, rows, chans = cots_ref.shape
    blocks = rows // TILE
    longest = masks_ref.shape[0] // 2
    count = 2 * evens * blocks
    before = before_ref[...] * masks_ref[1, 0:1, :]
    sources = [block[at : at + TILE] for block in (before, flipped_ref[...]) for at in range(0, rows, TILE)]
    for n, tile in enumerate(sources[::-1]):
        sources_ref[n * TILE : (n + 1) * TILE, :] = tile
    zero = jnp.zeros((TILE, chans), BF16)
    wide = []
    for e in range(evens):
        cots = cots_ref[e] if e == 0 else cots_ref[e] * masks_ref[longest + 2 * e, 0:1, :]
        tiles = [zero] + [cots[at : at + TILE] for at in range(0, rows, TILE)] + [zero]
        wide += [jnp.concatenate(tiles[n : n + 2], axis=1) for n in range(blocks + 1)]
    wide = jnp.concatenate(wide, axis=0)
    sums = [None] * count
    for x in range(0, 2 * blocks, 2):
        source = jnp.concatenate(sources[x : x + 2], axis=1)
        product = lax.dot_general(source, wide, (((1,), (1,)), ((), ())), preferred_element_type=F32)
        for e in range(evens):
            for n in range(blocks + 1):
                d = 2 * blocks * e + n - 1 + blocks - x
                if d >= 0:
                    at = (e * (blocks + 1) + n) * TILE
                    piece = product[:, at : at + TILE]
                    sums[d] = piece if sums[d] is None else sums[d] + piece
    row = lax.broadcasted_iota(jnp.int32, (TILE, TILE), 0)
    col = lax.broadcasted_iota(jnp.int32, (TILE, TILE), 1)
    sums[0] = jnp.where(row + col >= TILE - 1, sums[0], 0.0)
    width = count * TILE
    skewed = pltpu.roll(jnp.concatenate(sums, axis=1), width - TILE + 1, 1, stride=1, stride_axis=0)
    lags = jnp.sum(skewed, axis=0, keepdims=True) * scale
    for p in range(width // owned):
        piece = lags[:, p * owned : (p + 1) * owned]
        for q in range(copies):
            parts_ref[p * copies + q, :, :owned] = piece


def ahead_kernel(masks_ref, taps_ref, sources_ref, later_ref, earlier_ref, ahead_ref):
    width = taps_ref.shape[1]
    count = sources_ref.shape[0] // TILE
    longest = masks_ref.shape[0] // 2
    rounded = taps_ref[...].astype(BF16).astype(F32)
    skewed = pltpu.roll(jnp.broadcast_to(rounded, (TILE, width)), 0, 1, stride=1, stride_axis=0)
    flip = flip_matrix()
    for d in range(width // TILE):
        block = skewed[:, d * TILE : (d + 1) * TILE]
        if d == 0:
            row = lax.broadcasted_iota(jnp.int32, block.shape, 0)
            col = lax.broadcasted_iota(jnp.int32, block.shape, 1)
            block = jnp.where(col >= row, block, 0.0)
        block = block.astype(BF16)
        later_ref[:, d * TILE : (d + 1) * TILE] = block
        earlier_ref[:, d * TILE : (d + 1) * TILE] = lax.dot_general(
            block, flip, (((0,), (0,)), ((), ())), preferred_element_type=F32
        ).astype(BF16)
    for m in range(1, longest // 2):
        mask = masks_ref[longest + 2 * m, 0:1, :]
        for b in range(count // 2):
            first = m * count + b + 1 - count // 2
            part = jnp.dot(
                earlier_ref[:, first * TILE : (first + count) * TILE], sources_ref[...], preferred_element_type=F32
            )
            ahead_ref[m - 1, b * TILE : (b + 1) * TILE, :] = part.astype(BF16) * mask


def near_kernel(
    masks_ref, value_ref, gate_in_ref, skip_ref, later_ref, earlier_ref, sources_ref, cots_ref,
    near_ref, grad_value_ref, grad_gate_ref, future_ref,
):
    longest, rows, _ = cots_ref.shape
    blocks = rows // TILE
    for k in range(longest):
        block = cots_ref[k] if k == 0 else cots_ref[k] * masks_ref[longest + k, 0:1, :]
        future_ref[k * rows : (k + 1) * rows, :] = block
    skip = skip_ref[...]
    for b in range(blocks):
        here = slice(b * TILE, (b + 1) * TILE)
        transposed = jnp.dot(
            later_ref[:, : (longest * blocks - b) * TILE], future_ref[b * TILE :, :], preferred_element_type=F32
        )
        through = transposed + skip * cots_ref[0, here, :].astype(F32)
        gate_in, value = gate_in_ref[here, :].astype(F32), value_ref[here, :].astype(F32)
        grad_value_ref[here, :] = (through * gate_in).astype(BF16)
        grad_gate_ref[here, :] = (through * value).astype(BF16)
        newer = blocks - 1 - b
        convolved = jnp.dot(
            earlier_ref[:, : (2 * blocks - newer) * TILE], sources_ref[newer * TILE :, :], preferred_element_type=F32
        )
        near_ref[here, :] = convolved + skip * (gate_in * value).astype(BF16).astype(F32)


def sum_kernel(gathered_ref, layer_out_ref, total_ref):
    del layer_out_ref
    owned = total_ref.shape[1]
    total_ref[...] = jnp.sum(gathered_ref[:, 0, :], axis=0, keepdims=True)[:, :owned]


PARAMS = pltpu.CompilerParams(vmem_limit_bytes=LIMIT)
VMEM = pl.BlockSpec(memory_space=pltpu.VMEM)
SMEM = pl.BlockSpec(memory_space=pltpu.SMEM)


def body(value_proj, gate_in, gate_out, skip_gain, filter_taps, doc_lengths, cotangent):
    rows, chans = value_proj.shape
    maxlag = filter_taps.shape[0]
    longest = maxlag // rows
    shards, groups = lax.axis_size("seq"), lax.axis_size("ch")
    block = jax.ShapeDtypeStruct((rows, chans), BF16)
    cot_gated = (cotangent.astype(F32) * gate_out.astype(F32)).astype(BF16)
    gated = (gate_in.astype(F32) * value_proj.astype(F32)).astype(BF16)
    flipped = gated.reshape(rows // TILE, TILE, chans)[:, ::-1].reshape(rows, chans)

    future = cot_gated[None]
    span = longest
    while span > 2:
        span //= 2
        future = jnp.concatenate([future, shifted(future, "seq", -span)], axis=0)
    before = shifted(flipped, "seq", 1)
    bits = max(future.shape[0].bit_length() - 1, 1)
    order = sorted(range(future.shape[0]), key=lambda n: int(format(n, f"0{bits}b")[::-1], 2))
    evens = future if len(order) <= 2 else jnp.stack([future[n] for n in order])
    odds = shifted(evens, "seq", -1)
    future = jnp.stack([evens, odds], axis=1).reshape(longest, rows, chans)

    masks, gate, skip = pl.pallas_call(
        masks_kernel,
        out_shape=(
            jax.ShapeDtypeStruct((2 * longest, 16, chans), BF16), block, jax.ShapeDtypeStruct((1, chans), F32)
        ),
        in_specs=[SMEM, VMEM, VMEM],
        out_specs=(VMEM,) * 3,
        compiler_params=PARAMS,
        name="masks",
    )(doc_lengths, gate_out, skip_gain.reshape(1, chans))

    owned = maxlag // shards
    grad_scale = 1.0 / math.sqrt(shards * rows * chans * groups)
    parts, sources = pl.pallas_call(
        functools.partial(lag_kernel, owned=owned, copies=groups, scale=grad_scale),
        out_shape=(
            jax.ShapeDtypeStruct((shards * groups, 1, -(-owned // TILE) * TILE), F32),
            jax.ShapeDtypeStruct((2 * rows, chans), BF16),
        ),
        in_specs=[VMEM] * 4,
        out_specs=(VMEM,) * 2,
        compiler_params=PARAMS,
        cost_estimate=pl.CostEstimate(flops=LAGF, bytes_accessed=2**20, transcendentals=0),
        name="lags",
    )(masks, flipped, before, evens)
    gathered = lax.all_to_all(parts, ("seq", "ch"), 0, 0, tiled=True)

    band = jax.ShapeDtypeStruct((TILE, maxlag), BF16)
    further = longest // 2 - 1
    later, earlier, ahead = pl.pallas_call(
        ahead_kernel,
        out_shape=(band, band, jax.ShapeDtypeStruct((further, rows, chans), BF16)),
        in_specs=[VMEM] * 3,
        out_specs=(VMEM,) * 3,
        compiler_params=PARAMS,
        name="ahead",
    )(masks, filter_taps.reshape(1, maxlag), sources)
    far = sum(shifted(ahead[m], "seq", 2 * m + 2).astype(F32) for m in range(further))

    near, grad_value, grad_gate = pl.pallas_call(
        near_kernel,
        out_shape=(jax.ShapeDtypeStruct((rows, chans), F32), block, block),
        in_specs=[VMEM] * 8,
        out_specs=(VMEM,) * 3,
        scratch_shapes=[pltpu.VMEM((maxlag, chans), BF16)],
        compiler_params=PARAMS,
        cost_estimate=pl.CostEstimate(flops=CONVF, bytes_accessed=2**20, transcendentals=0),
        name="near",
    )(masks, value_proj, gate_in, skip, later, earlier, sources, future)
    layer_out = (gate.astype(F32) * (near + far)).astype(BF16)
    filter_grad = pl.pallas_call(
        sum_kernel,
        out_shape=jax.ShapeDtypeStruct((1, owned), F32),
        in_specs=[VMEM, pl.BlockSpec(memory_space=pl.ANY)],
        out_specs=VMEM,
        compiler_params=PARAMS,
        name="sum",
    )(gathered, layer_out)[0]
    return (layer_out, grad_value, grad_gate, filter_grad)


def solution(mesh):
    placed = (P("seq", "ch"), P("seq", "ch"), P("seq", "ch"), P("ch"), P(), P(), P("seq", "ch"))
    return jax.shard_map(
        body,
        mesh=mesh,
        in_specs=placed,
        out_specs=(P("seq", "ch"), P("seq", "ch"), P("seq", "ch"), P("seq")),
        check_vma=False,
    )
```

```python
import functools
import math

import jax
import jax.numpy as jnp
from jax import lax
from jax.experimental import pallas as pl
from jax.experimental.pallas import tpu as pltpu
from jax.sharding import PartitionSpec as P

TILE = 128
LIMIT = 8 * 1024 * 1024
LAGF = 10**10
CONVF = 10**10
F32 = jnp.float32
BF16 = jnp.bfloat16


def shifted(value, axis, by):
    length = lax.axis_size(axis)
    pairs = [(i, i + by) for i in range(length) if 0 <= i + by < length]
    return lax.ppermute(value, axis, pairs)


def doc_masks(lengths_ref, offsets, chans):
    position = lax.axis_index("seq")
    lengths = lengths_ref[...]
    start = stop = end = jnp.zeros((1, chans), jnp.int32)
    for k in range(lengths.shape[1]):
        begin, end = end, end + jnp.broadcast_to(lengths[:, k : k + 1], end.shape)
        inside = jnp.logical_and(begin <= position, position < end)
        start, stop = jnp.where(inside, begin, start), jnp.where(inside, end, stop)
    masks = []
    for offset in offsets:
        inside = jnp.logical_and(start <= position + offset, position + offset < stop)
        masks.append(jnp.where(inside, 1.0, 0.0).astype(BF16))
    return masks


def flip_matrix():
    row = lax.broadcasted_iota(jnp.int32, (TILE, TILE), 0)
    col = lax.broadcasted_iota(jnp.int32, (TILE, TILE), 1)
    return (row + col == TILE - 1).astype(F32).astype(BF16)


def stage_kernel(lengths_ref, skip_ref, lengths_out_ref, skip_out_ref):
    lengths_out_ref[...] = lengths_ref[...]
    skip_out_ref[...] = skip_ref[...]


def lag_kernel(
    lengths_ref, flipped_ref, before_ref, cots_ref, gate_out_ref, parts_ref, sources_ref,
    *, owned, copies, scale,
):
    del gate_out_ref
    evens, rows, chans = cots_ref.shape
    blocks = rows // TILE
    count = 2 * evens * blocks
    masks = doc_masks(lengths_ref, [-1] + [2 * e for e in range(1, evens)], chans)
    before = before_ref[...] * masks[0]
    sources = [block[at : at + TILE] for block in (before, flipped_ref[...]) for at in range(0, rows, TILE)]
    for n, tile in enumerate(sources[::-1]):
        sources_ref[n * TILE : (n + 1) * TILE, :] = tile
    zero = jnp.zeros((TILE, chans), BF16)
    wide = []
    for e in range(evens):
        cots = cots_ref[e] if e == 0 else cots_ref[e] * masks[e]
        tiles = [zero] + [cots[at : at + TILE] for at in range(0, rows, TILE)] + [zero]
        wide += [jnp.concatenate(tiles[n : n + 2], axis=1) for n in range(blocks + 1)]
    wide = jnp.concatenate(wide, axis=0)
    sums = [None] * count
    for x in range(0, 2 * blocks, 2):
        source = jnp.concatenate(sources[x : x + 2], axis=1)
        product = lax.dot_general(source, wide, (((1,), (1,)), ((), ())), preferred_element_type=F32)
        for e in range(evens):
            for n in range(blocks + 1):
                d = 2 * blocks * e + n - 1 + blocks - x
                if d >= 0:
                    at = (e * (blocks + 1) + n) * TILE
                    piece = product[:, at : at + TILE]
                    sums[d] = piece if sums[d] is None else sums[d] + piece
    row = lax.broadcasted_iota(jnp.int32, (TILE, TILE), 0)
    col = lax.broadcasted_iota(jnp.int32, (TILE, TILE), 1)
    sums[0] = jnp.where(row + col >= TILE - 1, sums[0], 0.0)
    width = count * TILE
    skewed = pltpu.roll(jnp.concatenate(sums, axis=1), width - TILE + 1, 1, stride=1, stride_axis=0)
    lags = jnp.sum(skewed, axis=0, keepdims=True) * scale
    for p in range(width // owned):
        piece = lags[:, p * owned : (p + 1) * owned]
        for q in range(copies):
            parts_ref[p * copies + q, :, :owned] = piece


def ahead_kernel(lengths_ref, taps_ref, sources_ref, later_ref, earlier_ref, ahead_ref):
    width = taps_ref.shape[1]
    count = sources_ref.shape[0] // TILE
    further, _, chans = ahead_ref.shape
    masks = doc_masks(lengths_ref, [2 * m for m in range(1, further + 1)], chans)
    rounded = taps_ref[...].astype(BF16).astype(F32)
    skewed = pltpu.roll(jnp.broadcast_to(rounded, (TILE, width)), 0, 1, stride=1, stride_axis=0)
    flip = flip_matrix()
    for d in range(width // TILE):
        block = skewed[:, d * TILE : (d + 1) * TILE]
        if d == 0:
            row = lax.broadcasted_iota(jnp.int32, block.shape, 0)
            col = lax.broadcasted_iota(jnp.int32, block.shape, 1)
            block = jnp.where(col >= row, block, 0.0)
        block = block.astype(BF16)
        later_ref[:, d * TILE : (d + 1) * TILE] = block
        earlier_ref[:, d * TILE : (d + 1) * TILE] = lax.dot_general(
            block, flip, (((0,), (0,)), ((), ())), preferred_element_type=F32
        ).astype(BF16)
    for m in range(1, further + 1):
        for b in range(count // 2):
            first = m * count + b + 1 - count // 2
            part = jnp.dot(
                earlier_ref[:, first * TILE : (first + count) * TILE], sources_ref[...], preferred_element_type=F32
            )
            ahead_ref[m - 1, b * TILE : (b + 1) * TILE, :] = part.astype(BF16) * masks[m - 1]


def near_kernel(
    lengths_ref, value_ref, gate_in_ref, skip_ref, later_ref, earlier_ref, sources_ref, cots_ref,
    near_ref, grad_value_ref, grad_gate_ref, future_ref,
):
    longest, rows, chans = cots_ref.shape
    blocks = rows // TILE
    masks = doc_masks(lengths_ref, range(longest), chans)
    for k in range(longest):
        block = cots_ref[k] if k == 0 else cots_ref[k] * masks[k]
        future_ref[k * rows : (k + 1) * rows, :] = block
    skip = skip_ref[...]
    for b in range(blocks):
        here = slice(b * TILE, (b + 1) * TILE)
        transposed = jnp.dot(
            later_ref[:, : (longest * blocks - b) * TILE], future_ref[b * TILE :, :], preferred_element_type=F32
        )
        through = transposed + skip * cots_ref[0, here, :].astype(F32)
        gate_in, value = gate_in_ref[here, :].astype(F32), value_ref[here, :].astype(F32)
        grad_value_ref[here, :] = (through * gate_in).astype(BF16)
        grad_gate_ref[here, :] = (through * value).astype(BF16)
        newer = blocks - 1 - b
        convolved = jnp.dot(
            earlier_ref[:, : (2 * blocks - newer) * TILE], sources_ref[newer * TILE :, :], preferred_element_type=F32
        )
        near_ref[here, :] = convolved + skip * (gate_in * value).astype(BF16).astype(F32)


def sum_kernel(gathered_ref, layer_out_ref, total_ref):
    del layer_out_ref
    owned = total_ref.shape[1]
    total_ref[...] = jnp.sum(gathered_ref[:, 0, :], axis=0, keepdims=True)[:, :owned]


PARAMS = pltpu.CompilerParams(vmem_limit_bytes=LIMIT)
VMEM = pl.BlockSpec(memory_space=pltpu.VMEM)


def body(value_proj, gate_in, gate_out, skip_gain, filter_taps, doc_lengths, cotangent):
    rows, chans = value_proj.shape
    maxlag = filter_taps.shape[0]
    longest = maxlag // rows
    shards, groups = lax.axis_size("seq"), lax.axis_size("ch")
    block = jax.ShapeDtypeStruct((rows, chans), BF16)
    cot_gated = (cotangent.astype(F32) * gate_out.astype(F32)).astype(BF16)
    gated = (gate_in.astype(F32) * value_proj.astype(F32)).astype(BF16)
    flipped = gated.reshape(rows // TILE, TILE, chans)[:, ::-1].reshape(rows, chans)

    future = cot_gated[None]
    span = longest
    while span > 2:
        span //= 2
        future = jnp.concatenate([future, shifted(future, "seq", -span)], axis=0)
    before = shifted(flipped, "seq", 1)
    bits = max(future.shape[0].bit_length() - 1, 1)
    order = sorted(range(future.shape[0]), key=lambda n: int(format(n, f"0{bits}b")[::-1], 2))
    evens = future if len(order) <= 2 else jnp.stack([future[n] for n in order])
    odds = shifted(evens, "seq", -1)
    future = jnp.stack([evens, odds], axis=1).reshape(longest, rows, chans)

    lengths, skip = pl.pallas_call(
        stage_kernel,
        out_shape=(
            jax.ShapeDtypeStruct((1, doc_lengths.shape[0]), jnp.int32), jax.ShapeDtypeStruct((1, chans), F32)
        ),
        in_specs=[VMEM] * 2,
        out_specs=(VMEM,) * 2,
        compiler_params=PARAMS,
        name="stage",
    )(doc_lengths.reshape(1, -1), skip_gain.reshape(1, chans))
    owned = maxlag // shards
    grad_scale = 1.0 / math.sqrt(shards * rows * chans * groups)
    parts, sources = pl.pallas_call(
        functools.partial(lag_kernel, owned=owned, copies=groups, scale=grad_scale),
        out_shape=(
            jax.ShapeDtypeStruct((shards * groups, 1, -(-owned // TILE) * TILE), F32),
            jax.ShapeDtypeStruct((2 * rows, chans), BF16),
        ),
        in_specs=[VMEM] * 5,
        out_specs=(VMEM,) * 2,
        compiler_params=PARAMS,
        cost_estimate=pl.CostEstimate(flops=LAGF, bytes_accessed=2**20, transcendentals=0),
        name="lags",
    )(lengths, flipped, before, evens, gate_out)
    gathered = lax.all_to_all(parts, ("seq", "ch"), 0, 0, tiled=True)

    band = jax.ShapeDtypeStruct((TILE, maxlag), BF16)
    further = longest // 2 - 1
    later, earlier, ahead = pl.pallas_call(
        ahead_kernel,
        out_shape=(band, band, jax.ShapeDtypeStruct((further, rows, chans), BF16)),
        in_specs=[VMEM] * 3,
        out_specs=(VMEM,) * 3,
        compiler_params=PARAMS,
        name="ahead",
    )(lengths, filter_taps.reshape(1, maxlag), sources)
    far = sum(shifted(ahead[m], "seq", 2 * m + 2).astype(F32) for m in range(further))

    near, grad_value, grad_gate = pl.pallas_call(
        near_kernel,
        out_shape=(jax.ShapeDtypeStruct((rows, chans), F32), block, block),
        in_specs=[VMEM] * 8,
        out_specs=(VMEM,) * 3,
        scratch_shapes=[pltpu.VMEM((maxlag, chans), BF16)],
        compiler_params=PARAMS,
        cost_estimate=pl.CostEstimate(flops=CONVF, bytes_accessed=2**20, transcendentals=0),
        name="near",
    )(lengths, value_proj, gate_in, skip, later, earlier, sources, future)
    layer_out = (gate_out.astype(F32) * (near + far)).astype(BF16)
    filter_grad = pl.pallas_call(
        sum_kernel,
        out_shape=jax.ShapeDtypeStruct((1, owned), F32),
        in_specs=[VMEM, pl.BlockSpec(memory_space=pl.ANY)],
        out_specs=VMEM,
        compiler_params=PARAMS,
        name="sum",
    )(gathered, layer_out)[0]
    return (layer_out, grad_value, grad_gate, filter_grad)


def solution(mesh):
    placed = (P("seq", "ch"), P("seq", "ch"), P("seq", "ch"), P("ch"), P(), P(), P("seq", "ch"))
    return jax.shard_map(
        body,
        mesh=mesh,
        in_specs=placed,
        out_specs=(P("seq", "ch"), P("seq", "ch"), P("seq", "ch"), P("seq")),
        check_vma=False,
    )
```

```python
import functools
import math

import jax
import jax.numpy as jnp
from jax import lax
from jax.experimental import pallas as pl
from jax.experimental.pallas import tpu as pltpu
from jax.sharding import PartitionSpec as P

TILE = 128
LIMIT = 8 * 1024 * 1024
LAGF = 10**10
CONVF = 10**10
F32 = jnp.float32
BF16 = jnp.bfloat16


def shifted(value, axis, by):
    length = lax.axis_size(axis)
    pairs = [(i, i + by) for i in range(length) if 0 <= i + by < length]
    return lax.ppermute(value, axis, pairs)


def rotated(value, axis, by):
    length = lax.axis_size(axis)
    return lax.ppermute(value, axis, [(i, (i + by) % length) for i in range(length)])


def doc_masks(lengths_ref, offsets, chans):
    position = lax.axis_index("seq")
    lengths = lengths_ref[...]
    start = stop = end = jnp.zeros((1, chans), jnp.int32)
    for k in range(lengths.shape[1]):
        begin, end = end, end + jnp.broadcast_to(lengths[:, k : k + 1], end.shape)
        inside = jnp.logical_and(begin <= position, position < end)
        start, stop = jnp.where(inside, begin, start), jnp.where(inside, end, stop)
    masks = []
    for offset in offsets:
        inside = jnp.logical_and(start <= position + offset, position + offset < stop)
        masks.append(jnp.where(inside, 1.0, 0.0).astype(BF16))
    return masks


def flip_matrix():
    row = lax.broadcasted_iota(jnp.int32, (TILE, TILE), 0)
    col = lax.broadcasted_iota(jnp.int32, (TILE, TILE), 1)
    return (row + col == TILE - 1).astype(F32).astype(BF16)


def stage_kernel(lengths_ref, skip_ref, lengths_out_ref, skip_out_ref):
    lengths_out_ref[...] = lengths_ref[...]
    skip_out_ref[...] = skip_ref[...]


def lag_kernel(
    lengths_ref, flipped_ref, before_ref, cots_ref, gate_out_ref, parts_ref, sources_ref,
    *, owned, copies, scale, shards,
):
    del gate_out_ref
    evens, rows, chans = cots_ref.shape
    blocks = rows // TILE
    masks = doc_masks(lengths_ref, [-1] + [2 * e for e in range(1, evens)], chans)
    before = before_ref[...] * masks[0]
    sources = [block[at : at + TILE] for block in (before, flipped_ref[...]) for at in range(0, rows, TILE)]
    zero = jnp.zeros((chans, TILE), BF16)

    def write_parts(used):
        wide = []
        for e in range(used):
            cots = cots_ref[e] if e == 0 else cots_ref[e] * masks[e]
            tiles = [cots[at : at + TILE].astype(F32).T.astype(BF16) for at in range(0, rows, TILE)]
            tiles = [zero] + tiles + [zero]
            wide += [jnp.concatenate(tiles[n : n + 2], axis=0) for n in range(blocks + 1)]
        wide = jnp.concatenate(wide, axis=1)
        sums = [None] * (2 * used * blocks)
        for x in range(0, 2 * blocks, 2):
            source = jnp.concatenate(sources[x : x + 2], axis=1)
            product = jnp.dot(source, wide, preferred_element_type=F32)
            for e in range(used):
                for n in range(blocks + 1):
                    d = 2 * blocks * e + n - 1 + blocks - x
                    if d >= 0:
                        at = (e * (blocks + 1) + n) * TILE
                        piece = product[:, at : at + TILE]
                        sums[d] = piece if sums[d] is None else sums[d] + piece
        row = lax.broadcasted_iota(jnp.int32, (TILE, TILE), 0)
        col = lax.broadcasted_iota(jnp.int32, (TILE, TILE), 1)
        sums[0] = jnp.where(row + col >= TILE - 1, sums[0], 0.0)
        width = len(sums) * TILE
        skewed = pltpu.roll(jnp.concatenate(sums, axis=1), width - TILE + 1, 1, stride=1, stride_axis=0)
        lags = jnp.sum(skewed, axis=0, keepdims=True) * scale
        for p in range(parts_ref.shape[0] // copies):
            some = min(max(width - p * owned, 0), owned)
            pieces = [lags[:, p * owned : p * owned + some]] if some > 0 else []
            pieces += [jnp.zeros((1, owned - some), F32)] if some < owned else []
            piece = pieces[0] if len(pieces) == 1 else jnp.concatenate(pieces, axis=1)
            for q in range(copies):
                parts_ref[p * copies + q, :, :owned] = piece

    if evens == 1:
        write_parts(1)
    else:
        later = lax.axis_index("seq") + 2 < shards
        pl.when(later)(functools.partial(write_parts, evens))
        pl.when(jnp.logical_not(later))(functools.partial(write_parts, 1))
    for n, tile in enumerate(sources[::-1]):
        sources_ref[n * TILE : (n + 1) * TILE, :] = tile


def ahead_kernel(lengths_ref, taps_ref, sources_ref, later_ref, earlier_ref, ahead_ref):
    width = taps_ref.shape[1]
    count = sources_ref.shape[0] // TILE
    further, _, chans = ahead_ref.shape
    masks = doc_masks(lengths_ref, [2 * m for m in range(1, further + 1)], chans)
    rounded = taps_ref[...].astype(BF16).astype(F32)
    skewed = pltpu.roll(jnp.broadcast_to(rounded, (TILE, width)), 0, 1, stride=1, stride_axis=0)
    flip = flip_matrix()
    for d in range(width // TILE):
        block = skewed[:, d * TILE : (d + 1) * TILE]
        if d == 0:
            row = lax.broadcasted_iota(jnp.int32, block.shape, 0)
            col = lax.broadcasted_iota(jnp.int32, block.shape, 1)
            block = jnp.where(col >= row, block, 0.0)
        block = block.astype(BF16)
        later_ref[:, d * TILE : (d + 1) * TILE] = block
        earlier_ref[:, d * TILE : (d + 1) * TILE] = lax.dot_general(
            block, flip, (((0,), (0,)), ((), ())), preferred_element_type=F32
        ).astype(BF16)
    for m in range(1, further + 1):
        for b in range(count // 2):
            first = m * count + b + 1 - count // 2
            part = jnp.dot(
                earlier_ref[:, first * TILE : (first + count) * TILE], sources_ref[...], preferred_element_type=F32
            )
            ahead_ref[m - 1, b * TILE : (b + 1) * TILE, :] = part.astype(BF16) * masks[m - 1]


def near_kernel(
    lengths_ref, value_ref, gate_in_ref, skip_ref, later_ref, earlier_ref, sources_ref, cots_ref,
    near_ref, grad_value_ref, grad_gate_ref, future_ref,
):
    longest, rows, chans = cots_ref.shape
    blocks = rows // TILE
    masks = doc_masks(lengths_ref, range(longest), chans)
    for k in range(longest):
        block = cots_ref[k] if k == 0 else cots_ref[k] * masks[k]
        future_ref[k * rows : (k + 1) * rows, :] = block
    skip = skip_ref[...]
    for b in range(blocks):
        here = slice(b * TILE, (b + 1) * TILE)
        transposed = jnp.dot(
            later_ref[:, : (longest * blocks - b) * TILE], future_ref[b * TILE :, :], preferred_element_type=F32
        )
        through = transposed + skip * cots_ref[0, here, :].astype(F32)
        gate_in, value = gate_in_ref[here, :].astype(F32), value_ref[here, :].astype(F32)
        grad_value_ref[here, :] = (through * gate_in).astype(BF16)
        grad_gate_ref[here, :] = (through * value).astype(BF16)
        newer = blocks - 1 - b
        convolved = jnp.dot(
            earlier_ref[:, : (2 * blocks - newer) * TILE], sources_ref[newer * TILE :, :], preferred_element_type=F32
        )
        near_ref[here, :] = convolved + skip * (gate_in * value).astype(BF16).astype(F32)


def sum_kernel(gathered_ref, layer_out_ref, total_ref):
    del layer_out_ref
    owned = total_ref.shape[1]
    total_ref[...] = jnp.sum(gathered_ref[:, 0, :], axis=0, keepdims=True)[:, :owned]


PARAMS = pltpu.CompilerParams(vmem_limit_bytes=LIMIT)
VMEM = pl.BlockSpec(memory_space=pltpu.VMEM)


def body(value_proj, gate_in, gate_out, skip_gain, filter_taps, doc_lengths, cotangent):
    rows, chans = value_proj.shape
    maxlag = filter_taps.shape[0]
    longest = maxlag // rows
    shards, groups = lax.axis_size("seq"), lax.axis_size("ch")
    block = jax.ShapeDtypeStruct((rows, chans), BF16)
    cot_gated = (cotangent.astype(F32) * gate_out.astype(F32)).astype(BF16)
    gate_in, cot_gated = lax.optimization_barrier((gate_in, cot_gated))
    gated = (gate_in.astype(F32) * value_proj.astype(F32)).astype(BF16)
    flipped = gated.reshape(rows // TILE, TILE, chans)[:, ::-1].reshape(rows, chans)

    future = cot_gated[None]
    span = longest
    while span > 2:
        span //= 2
        future = jnp.concatenate([future, shifted(future, "seq", -span)], axis=0)
    before = rotated(flipped, "seq", 1)
    bits = max(future.shape[0].bit_length() - 1, 1)
    order = sorted(range(future.shape[0]), key=lambda n: int(format(n, f"0{bits}b")[::-1], 2))
    evens = future if len(order) <= 2 else jnp.stack([future[n] for n in order])
    odds = rotated(evens, "seq", -1)
    future = jnp.stack([evens, odds], axis=1).reshape(longest, rows, chans)

    lengths, skip = pl.pallas_call(
        stage_kernel,
        out_shape=(
            jax.ShapeDtypeStruct((1, doc_lengths.shape[0]), jnp.int32), jax.ShapeDtypeStruct((1, chans), F32)
        ),
        in_specs=[VMEM] * 2,
        out_specs=(VMEM,) * 2,
        compiler_params=PARAMS,
        name="stage",
    )(doc_lengths.reshape(1, -1), skip_gain.reshape(1, chans))
    owned = maxlag // shards
    grad_scale = 1.0 / math.sqrt(shards * rows * chans * groups)
    parts, sources = pl.pallas_call(
        functools.partial(lag_kernel, owned=owned, copies=groups, scale=grad_scale, shards=shards),
        out_shape=(
            jax.ShapeDtypeStruct((shards * groups, 1, -(-owned // TILE) * TILE), F32),
            jax.ShapeDtypeStruct((2 * rows, chans), BF16),
        ),
        in_specs=[VMEM] * 5,
        out_specs=(VMEM,) * 2,
        compiler_params=PARAMS,
        cost_estimate=pl.CostEstimate(flops=LAGF, bytes_accessed=2**20, transcendentals=0),
        name="lags",
    )(lengths, flipped, before, evens, gate_out)
    gathered = lax.all_to_all(parts, ("seq", "ch"), 0, 0, tiled=True)

    band = jax.ShapeDtypeStruct((TILE, maxlag), BF16)
    further = longest // 2 - 1
    later, earlier, ahead = pl.pallas_call(
        ahead_kernel,
        out_shape=(band, band, jax.ShapeDtypeStruct((further, rows, chans), BF16)),
        in_specs=[VMEM] * 3,
        out_specs=(VMEM,) * 3,
        compiler_params=PARAMS,
        name="ahead",
    )(lengths, filter_taps.reshape(1, maxlag), sources)
    far = sum(shifted(ahead[m], "seq", 2 * m + 2).astype(F32) for m in range(further))

    near, grad_value, grad_gate = pl.pallas_call(
        near_kernel,
        out_shape=(jax.ShapeDtypeStruct((rows, chans), F32), block, block),
        in_specs=[VMEM] * 8,
        out_specs=(VMEM,) * 3,
        scratch_shapes=[pltpu.VMEM((maxlag, chans), BF16)],
        compiler_params=PARAMS,
        cost_estimate=pl.CostEstimate(flops=CONVF, bytes_accessed=2**20, transcendentals=0),
        name="near",
    )(lengths, value_proj, gate_in, skip, later, earlier, sources, future)
    layer_out = (gate_out.astype(F32) * (near + far)).astype(BF16)
    filter_grad = pl.pallas_call(
        sum_kernel,
        out_shape=jax.ShapeDtypeStruct((1, owned), F32),
        in_specs=[VMEM, pl.BlockSpec(memory_space=pl.ANY)],
        out_specs=VMEM,
        compiler_params=PARAMS,
        name="sum",
    )(gathered, layer_out)[0]
    return (layer_out, grad_value, grad_gate, filter_grad)


def solution(mesh):
    placed = (P("seq", "ch"), P("seq", "ch"), P("seq", "ch"), P("ch"), P(), P(), P("seq", "ch"))
    return jax.shard_map(
        body,
        mesh=mesh,
        in_specs=placed,
        out_specs=(P("seq", "ch"), P("seq", "ch"), P("seq", "ch"), P("seq")),
        check_vma=False,
    )
```

```python
import functools
import math

import jax
import jax.numpy as jnp
from jax import lax
from jax.experimental import pallas as pl
from jax.experimental.pallas import tpu as pltpu
from jax.sharding import PartitionSpec as P

TILE = 128
LIMIT = 8 * 1024 * 1024
LAGF = 10**10
CONVF = 10**10
F32 = jnp.float32
BF16 = jnp.bfloat16


def shifted(value, axis, by):
    length = lax.axis_size(axis)
    pairs = [(i, i + by) for i in range(length) if 0 <= i + by < length]
    return lax.ppermute(value, axis, pairs)


def rotated(value, axis, by):
    length = lax.axis_size(axis)
    return lax.ppermute(value, axis, [(i, (i + by) % length) for i in range(length)])


def doc_masks(lengths_ref, offsets, chans):
    position = lax.axis_index("seq")
    lengths = lengths_ref[...]
    start = stop = end = jnp.zeros((1, chans), jnp.int32)
    for k in range(lengths.shape[1]):
        begin, end = end, end + jnp.broadcast_to(lengths[:, k : k + 1], end.shape)
        inside = jnp.logical_and(begin <= position, position < end)
        start, stop = jnp.where(inside, begin, start), jnp.where(inside, end, stop)
    masks = []
    for offset in offsets:
        inside = jnp.logical_and(start <= position + offset, position + offset < stop)
        masks.append(jnp.where(inside, 1.0, 0.0).astype(BF16))
    return masks


def flip_matrix():
    row = lax.broadcasted_iota(jnp.int32, (TILE, TILE), 0)
    col = lax.broadcasted_iota(jnp.int32, (TILE, TILE), 1)
    return (row + col == TILE - 1).astype(F32).astype(BF16)


def stage_kernel(lengths_ref, skip_ref, cots_ref, lengths_out_ref, skip_out_ref, turned_ref, masks_ref):
    lengths_out_ref[...] = lengths_ref[...]
    skip_out_ref[...] = skip_ref[...]
    rows, chans = cots_ref.shape
    for at in range(0, rows, TILE):
        turned_ref[:, at : at + TILE] = cots_ref[at : at + TILE, :].astype(F32).T.astype(BF16)
    evens = masks_ref.shape[0]
    for n, mask in enumerate(doc_masks(lengths_ref, [-1] + [2 * e for e in range(1, evens)], chans)):
        masks_ref[n] = jnp.broadcast_to(mask.astype(F32), masks_ref.shape[1:])


def lag_kernel(
    masks_ref, flipped_ref, before_ref, turned_ref, cots_ref, gate_out_ref, parts_ref, sources_ref,
    *, owned, copies, scale, shards,
):
    del gate_out_ref
    evens, rows, chans = cots_ref.shape
    blocks = rows // TILE
    masks = [masks_ref[n, 0:1, :].astype(BF16) for n in range(evens)]
    before = before_ref[...] * masks[0]
    sources = [block[at : at + TILE] for block in (before, flipped_ref[...]) for at in range(0, rows, TILE)]
    zero = jnp.zeros((chans, TILE), BF16)

    def write_parts(used):
        wide = []
        for e in range(used):
            if e == 0:
                tiles = [turned_ref[:, at : at + TILE] for at in range(0, rows, TILE)]
            else:
                cots = cots_ref[e] * masks[e]
                tiles = [cots[at : at + TILE].astype(F32).T.astype(BF16) for at in range(0, rows, TILE)]
            tiles = [zero] + tiles + [zero]
            wide += [jnp.concatenate(tiles[n : n + 2], axis=0) for n in range(blocks + 1)]
        wide = jnp.concatenate(wide, axis=1)
        sums = [None] * (2 * used * blocks)
        for x in range(0, 2 * blocks, 2):
            source = jnp.concatenate(sources[x : x + 2], axis=1)
            product = jnp.dot(source, wide, preferred_element_type=F32)
            for e in range(used):
                for n in range(blocks + 1):
                    d = 2 * blocks * e + n - 1 + blocks - x
                    if d >= 0:
                        at = (e * (blocks + 1) + n) * TILE
                        piece = product[:, at : at + TILE]
                        sums[d] = piece if sums[d] is None else sums[d] + piece
        row = lax.broadcasted_iota(jnp.int32, (TILE, TILE), 0)
        col = lax.broadcasted_iota(jnp.int32, (TILE, TILE), 1)
        sums[0] = jnp.where(row + col >= TILE - 1, sums[0], 0.0)
        width = len(sums) * TILE
        skewed = pltpu.roll(jnp.concatenate(sums, axis=1), width - TILE + 1, 1, stride=1, stride_axis=0)
        lags = jnp.sum(skewed, axis=0, keepdims=True) * scale
        for p in range(parts_ref.shape[0] // copies):
            some = min(max(width - p * owned, 0), owned)
            pieces = [lags[:, p * owned : p * owned + some]] if some > 0 else []
            pieces += [jnp.zeros((1, owned - some), F32)] if some < owned else []
            piece = pieces[0] if len(pieces) == 1 else jnp.concatenate(pieces, axis=1)
            for q in range(copies):
                parts_ref[p * copies + q, :, :owned] = piece

    if evens == 1:
        write_parts(1)
    else:
        later = lax.axis_index("seq") + 2 < shards
        pl.when(later)(functools.partial(write_parts, evens))
        pl.when(jnp.logical_not(later))(functools.partial(write_parts, 1))
    for n, tile in enumerate(sources[::-1]):
        sources_ref[n * TILE : (n + 1) * TILE, :] = tile


def ahead_kernel(lengths_ref, taps_ref, sources_ref, later_ref, earlier_ref, ahead_ref):
    width = taps_ref.shape[1]
    count = sources_ref.shape[0] // TILE
    further, _, chans = ahead_ref.shape
    masks = doc_masks(lengths_ref, [2 * m for m in range(1, further + 1)], chans)
    rounded = taps_ref[...].astype(BF16).astype(F32)
    skewed = pltpu.roll(jnp.broadcast_to(rounded, (TILE, width)), 0, 1, stride=1, stride_axis=0)
    flip = flip_matrix()
    for d in range(width // TILE):
        block = skewed[:, d * TILE : (d + 1) * TILE]
        if d == 0:
            row = lax.broadcasted_iota(jnp.int32, block.shape, 0)
            col = lax.broadcasted_iota(jnp.int32, block.shape, 1)
            block = jnp.where(col >= row, block, 0.0)
        block = block.astype(BF16)
        later_ref[:, d * TILE : (d + 1) * TILE] = block
        earlier_ref[:, d * TILE : (d + 1) * TILE] = lax.dot_general(
            block, flip, (((0,), (0,)), ((), ())), preferred_element_type=F32
        ).astype(BF16)
    for m in range(1, further + 1):
        for b in range(count // 2):
            first = m * count + b + 1 - count // 2
            part = jnp.dot(
                earlier_ref[:, first * TILE : (first + count) * TILE], sources_ref[...], preferred_element_type=F32
            )
            ahead_ref[m - 1, b * TILE : (b + 1) * TILE, :] = part.astype(BF16) * masks[m - 1]


def near_kernel(
    lengths_ref, value_ref, gate_in_ref, skip_ref, later_ref, earlier_ref, sources_ref, cots_ref,
    near_ref, grad_value_ref, grad_gate_ref, future_ref,
):
    longest, rows, chans = cots_ref.shape
    blocks = rows // TILE
    masks = doc_masks(lengths_ref, range(longest), chans)
    for k in range(longest):
        block = cots_ref[k] if k == 0 else cots_ref[k] * masks[k]
        future_ref[k * rows : (k + 1) * rows, :] = block
    skip = skip_ref[...]
    for b in range(blocks):
        here = slice(b * TILE, (b + 1) * TILE)
        transposed = jnp.dot(
            later_ref[:, : (longest * blocks - b) * TILE], future_ref[b * TILE :, :], preferred_element_type=F32
        )
        through = transposed + skip * cots_ref[0, here, :].astype(F32)
        gate_in, value = gate_in_ref[here, :].astype(F32), value_ref[here, :].astype(F32)
        grad_value_ref[here, :] = (through * gate_in).astype(BF16)
        grad_gate_ref[here, :] = (through * value).astype(BF16)
        newer = blocks - 1 - b
        convolved = jnp.dot(
            earlier_ref[:, : (2 * blocks - newer) * TILE], sources_ref[newer * TILE :, :], preferred_element_type=F32
        )
        near_ref[here, :] = convolved + skip * (gate_in * value).astype(BF16).astype(F32)


def sum_kernel(gathered_ref, layer_out_ref, total_ref):
    del layer_out_ref
    owned = total_ref.shape[1]
    total_ref[...] = jnp.sum(gathered_ref[:, 0, :], axis=0, keepdims=True)[:, :owned]


PARAMS = pltpu.CompilerParams(vmem_limit_bytes=LIMIT)
VMEM = pl.BlockSpec(memory_space=pltpu.VMEM)


def body(value_proj, gate_in, gate_out, skip_gain, filter_taps, doc_lengths, cotangent):
    rows, chans = value_proj.shape
    maxlag = filter_taps.shape[0]
    longest = maxlag // rows
    shards, groups = lax.axis_size("seq"), lax.axis_size("ch")
    block = jax.ShapeDtypeStruct((rows, chans), BF16)
    cot_gated = (cotangent.astype(F32) * gate_out.astype(F32)).astype(BF16)
    gated = (gate_in.astype(F32) * value_proj.astype(F32)).astype(BF16)
    flipped = gated.reshape(rows // TILE, TILE, chans)[:, ::-1].reshape(rows, chans)

    future = cot_gated[None]
    span = longest
    while span > 2:
        span //= 2
        future = jnp.concatenate([future, shifted(future, "seq", -span)], axis=0)
    before = rotated(flipped, "seq", 1)
    bits = max(future.shape[0].bit_length() - 1, 1)
    order = sorted(range(future.shape[0]), key=lambda n: int(format(n, f"0{bits}b")[::-1], 2))
    evens = future if len(order) <= 2 else jnp.stack([future[n] for n in order])
    odds = rotated(evens, "seq", -1)
    future = jnp.stack([evens, odds], axis=1).reshape(longest, rows, chans)

    lengths, skip, turned, masks = pl.pallas_call(
        stage_kernel,
        out_shape=(
            jax.ShapeDtypeStruct((1, doc_lengths.shape[0]), jnp.int32),
            jax.ShapeDtypeStruct((1, chans), F32),
            jax.ShapeDtypeStruct((chans, rows), BF16),
            jax.ShapeDtypeStruct((evens.shape[0], 8, chans), F32),
        ),
        in_specs=[VMEM] * 3,
        out_specs=(VMEM,) * 4,
        compiler_params=PARAMS,
        name="stage",
    )(doc_lengths.reshape(1, -1), skip_gain.reshape(1, chans), cot_gated)
    owned = maxlag // shards
    grad_scale = 1.0 / math.sqrt(shards * rows * chans * groups)
    parts, sources = pl.pallas_call(
        functools.partial(lag_kernel, owned=owned, copies=groups, scale=grad_scale, shards=shards),
        out_shape=(
            jax.ShapeDtypeStruct((shards * groups, 1, -(-owned // TILE) * TILE), F32),
            jax.ShapeDtypeStruct((2 * rows, chans), BF16),
        ),
        in_specs=[VMEM] * 6,
        out_specs=(VMEM,) * 2,
        compiler_params=PARAMS,
        cost_estimate=pl.CostEstimate(flops=LAGF, bytes_accessed=2**20, transcendentals=0),
        name="lags",
    )(masks, flipped, before, turned, evens, gate_out)
    gathered = lax.all_to_all(parts, ("seq", "ch"), 0, 0, tiled=True)

    band = jax.ShapeDtypeStruct((TILE, maxlag), BF16)
    further = longest // 2 - 1
    later, earlier, ahead = pl.pallas_call(
        ahead_kernel,
        out_shape=(band, band, jax.ShapeDtypeStruct((further, rows, chans), BF16)),
        in_specs=[VMEM] * 3,
        out_specs=(VMEM,) * 3,
        compiler_params=PARAMS,
        name="ahead",
    )(lengths, filter_taps.reshape(1, maxlag), sources)
    far = sum(shifted(ahead[m], "seq", 2 * m + 2).astype(F32) for m in range(further))

    near, grad_value, grad_gate = pl.pallas_call(
        near_kernel,
        out_shape=(jax.ShapeDtypeStruct((rows, chans), F32), block, block),
        in_specs=[VMEM] * 8,
        out_specs=(VMEM,) * 3,
        scratch_shapes=[pltpu.VMEM((maxlag, chans), BF16)],
        compiler_params=PARAMS,
        cost_estimate=pl.CostEstimate(flops=CONVF, bytes_accessed=2**20, transcendentals=0),
        name="near",
    )(lengths, value_proj, gate_in, skip, later, earlier, sources, future)
    layer_out = (gate_out.astype(F32) * (near + far)).astype(BF16)
    filter_grad = pl.pallas_call(
        sum_kernel,
        out_shape=jax.ShapeDtypeStruct((1, owned), F32),
        in_specs=[VMEM, pl.BlockSpec(memory_space=pl.ANY)],
        out_specs=VMEM,
        compiler_params=PARAMS,
        name="sum",
    )(gathered, layer_out)[0]
    return (layer_out, grad_value, grad_gate, filter_grad)


def solution(mesh):
    placed = (P("seq", "ch"), P("seq", "ch"), P("seq", "ch"), P("ch"), P(), P(), P("seq", "ch"))
    return jax.shard_map(
        body,
        mesh=mesh,
        in_specs=placed,
        out_specs=(P("seq", "ch"), P("seq", "ch"), P("seq", "ch"), P("seq")),
        check_vma=False,
    )
```

```python
import functools
import math

import jax
import jax.numpy as jnp
from jax import lax
from jax.experimental import pallas as pl
from jax.experimental.pallas import tpu as pltpu
from jax.sharding import PartitionSpec as P

TILE = 128
LIMIT = 8 * 1024 * 1024
LAGF = 10**10
CONVF = 10**10
F32 = jnp.float32
BF16 = jnp.bfloat16


def shifted(value, axis, by):
    length = lax.axis_size(axis)
    pairs = [(i, i + by) for i in range(length) if 0 <= i + by < length]
    return lax.ppermute(value, axis, pairs)


def rotated(value, axis, by):
    length = lax.axis_size(axis)
    return lax.ppermute(value, axis, [(i, (i + by) % length) for i in range(length)])


def doc_masks(lengths_ref, offsets, chans):
    position = lax.axis_index("seq")
    lengths = lengths_ref[...]
    start = stop = end = jnp.zeros((1, chans), jnp.int32)
    for k in range(lengths.shape[1]):
        begin, end = end, end + jnp.broadcast_to(lengths[:, k : k + 1], end.shape)
        inside = jnp.logical_and(begin <= position, position < end)
        start, stop = jnp.where(inside, begin, start), jnp.where(inside, end, stop)
    masks = []
    for offset in offsets:
        inside = jnp.logical_and(start <= position + offset, position + offset < stop)
        masks.append(jnp.where(inside, 1.0, 0.0).astype(BF16))
    return masks


def flip_matrix():
    row = lax.broadcasted_iota(jnp.int32, (TILE, TILE), 0)
    col = lax.broadcasted_iota(jnp.int32, (TILE, TILE), 1)
    return (row + col == TILE - 1).astype(F32).astype(BF16)


def stage_kernel(lengths_ref, skip_ref, cots_ref, lengths_out_ref, skip_out_ref, turned_ref, masks_ref):
    lengths_out_ref[...] = lengths_ref[...]
    skip_out_ref[...] = skip_ref[...]
    rows, chans = cots_ref.shape
    for at in range(0, rows, TILE):
        turned_ref[:, at : at + TILE] = cots_ref[at : at + TILE, :].astype(F32).T.astype(BF16)
    evens = masks_ref.shape[0]
    for n, mask in enumerate(doc_masks(lengths_ref, [-1] + [2 * e for e in range(1, evens)], chans)):
        masks_ref[n] = jnp.broadcast_to(mask.astype(F32), masks_ref.shape[1:])


def lag_kernel(
    masks_ref, flipped_ref, before_ref, turned_ref, cots_ref, gate_out_ref, parts_ref, sources_ref,
    *, owned, copies, scale, shards,
):
    del gate_out_ref
    evens, rows, chans = cots_ref.shape
    blocks = rows // TILE
    masks = [masks_ref[n, 0:1, :].astype(BF16) for n in range(evens)]
    before = before_ref[...] * masks[0]
    sources = [block[at : at + TILE] for block in (before, flipped_ref[...]) for at in range(0, rows, TILE)]
    zero = jnp.zeros((chans, TILE), BF16)

    def write_parts(used):
        wide = []
        for e in range(used):
            if e == 0:
                tiles = [turned_ref[:, at : at + TILE] for at in range(0, rows, TILE)]
            else:
                cots = cots_ref[e] * masks[e]
                tiles = [cots[at : at + TILE].astype(F32).T.astype(BF16) for at in range(0, rows, TILE)]
            tiles = [zero] + tiles + [zero]
            wide += [jnp.concatenate(tiles[n : n + 2], axis=0) for n in range(blocks + 1)]
        wide = jnp.concatenate(wide, axis=1)
        sums = [None] * (2 * used * blocks)
        for x in range(0, 2 * blocks, 2):
            source = jnp.concatenate(sources[x : x + 2], axis=1)
            product = jnp.dot(source, wide, preferred_element_type=F32)
            for e in range(used):
                for n in range(blocks + 1):
                    d = 2 * blocks * e + n - 1 + blocks - x
                    if d >= 0:
                        at = (e * (blocks + 1) + n) * TILE
                        piece = product[:, at : at + TILE]
                        sums[d] = piece if sums[d] is None else sums[d] + piece
        row = lax.broadcasted_iota(jnp.int32, (TILE, TILE), 0)
        col = lax.broadcasted_iota(jnp.int32, (TILE, TILE), 1)
        sums[0] = jnp.where(row + col >= TILE - 1, sums[0], 0.0)
        width = len(sums) * TILE
        skewed = pltpu.roll(jnp.concatenate(sums, axis=1), width - TILE + 1, 1, stride=1, stride_axis=0)
        lags = jnp.sum(skewed, axis=0, keepdims=True) * scale
        for p in range(parts_ref.shape[0] // copies):
            some = min(max(width - p * owned, 0), owned)
            pieces = [lags[:, p * owned : p * owned + some]] if some > 0 else []
            pieces += [jnp.zeros((1, owned - some), F32)] if some < owned else []
            piece = pieces[0] if len(pieces) == 1 else jnp.concatenate(pieces, axis=1)
            for q in range(copies):
                parts_ref[q * shards + p, :, :owned] = piece

    if evens == 1:
        write_parts(1)
    else:
        later = lax.axis_index("seq") + 2 < shards
        pl.when(later)(functools.partial(write_parts, evens))
        pl.when(jnp.logical_not(later))(functools.partial(write_parts, 1))
    for n, tile in enumerate(sources[::-1]):
        sources_ref[n * TILE : (n + 1) * TILE, :] = tile


def ahead_kernel(lengths_ref, taps_ref, sources_ref, later_ref, earlier_ref, ahead_ref):
    width = taps_ref.shape[1]
    count = sources_ref.shape[0] // TILE
    further, _, chans = ahead_ref.shape
    masks = doc_masks(lengths_ref, [2 * m for m in range(1, further + 1)], chans)
    rounded = taps_ref[...].astype(BF16).astype(F32)
    skewed = pltpu.roll(jnp.broadcast_to(rounded, (TILE, width)), 0, 1, stride=1, stride_axis=0)
    flip = flip_matrix()
    for d in range(width // TILE):
        block = skewed[:, d * TILE : (d + 1) * TILE]
        if d == 0:
            row = lax.broadcasted_iota(jnp.int32, block.shape, 0)
            col = lax.broadcasted_iota(jnp.int32, block.shape, 1)
            block = jnp.where(col >= row, block, 0.0)
        block = block.astype(BF16)
        later_ref[:, d * TILE : (d + 1) * TILE] = block
        earlier_ref[:, d * TILE : (d + 1) * TILE] = lax.dot_general(
            block, flip, (((0,), (0,)), ((), ())), preferred_element_type=F32
        ).astype(BF16)
    for m in range(1, further + 1):
        for b in range(count // 2):
            first = m * count + b + 1 - count // 2
            part = jnp.dot(
                earlier_ref[:, first * TILE : (first + count) * TILE], sources_ref[...], preferred_element_type=F32
            )
            ahead_ref[m - 1, b * TILE : (b + 1) * TILE, :] = part.astype(BF16) * masks[m - 1]


def near_kernel(
    lengths_ref, value_ref, gate_in_ref, skip_ref, later_ref, earlier_ref, sources_ref, cots_ref,
    near_ref, grad_value_ref, grad_gate_ref, future_ref,
):
    longest, rows, chans = cots_ref.shape
    blocks = rows // TILE
    masks = doc_masks(lengths_ref, range(longest), chans)
    for k in range(longest):
        block = cots_ref[k] if k == 0 else cots_ref[k] * masks[k]
        future_ref[k * rows : (k + 1) * rows, :] = block
    skip = skip_ref[...]
    for b in range(blocks):
        here = slice(b * TILE, (b + 1) * TILE)
        transposed = jnp.dot(
            later_ref[:, : (longest * blocks - b) * TILE], future_ref[b * TILE :, :], preferred_element_type=F32
        )
        through = transposed + skip * cots_ref[0, here, :].astype(F32)
        gate_in, value = gate_in_ref[here, :].astype(F32), value_ref[here, :].astype(F32)
        grad_value_ref[here, :] = (through * gate_in).astype(BF16)
        grad_gate_ref[here, :] = (through * value).astype(BF16)
        newer = blocks - 1 - b
        convolved = jnp.dot(
            earlier_ref[:, : (2 * blocks - newer) * TILE], sources_ref[newer * TILE :, :], preferred_element_type=F32
        )
        near_ref[here, :] = convolved + skip * (gate_in * value).astype(BF16).astype(F32)


def sum_kernel(gathered_ref, layer_out_ref, total_ref):
    del layer_out_ref
    owned = total_ref.shape[1]
    total_ref[...] = jnp.sum(gathered_ref[:, 0, :], axis=0, keepdims=True)[:, :owned]


PARAMS = pltpu.CompilerParams(vmem_limit_bytes=LIMIT)
VMEM = pl.BlockSpec(memory_space=pltpu.VMEM)


def body(value_proj, gate_in, gate_out, skip_gain, filter_taps, doc_lengths, cotangent):
    rows, chans = value_proj.shape
    maxlag = filter_taps.shape[0]
    longest = maxlag // rows
    shards, groups = lax.axis_size("seq"), lax.axis_size("ch")
    block = jax.ShapeDtypeStruct((rows, chans), BF16)
    cot_gated = (cotangent.astype(F32) * gate_out.astype(F32)).astype(BF16)
    gated = (gate_in.astype(F32) * value_proj.astype(F32)).astype(BF16)
    flipped = gated.reshape(rows // TILE, TILE, chans)[:, ::-1].reshape(rows, chans)

    future = cot_gated[None]
    span = longest
    while span > 2:
        span //= 2
        future = jnp.concatenate([future, shifted(future, "seq", -span)], axis=0)
    before = rotated(flipped, "seq", 1)
    bits = max(future.shape[0].bit_length() - 1, 1)
    order = sorted(range(future.shape[0]), key=lambda n: int(format(n, f"0{bits}b")[::-1], 2))
    evens = future if len(order) <= 2 else jnp.stack([future[n] for n in order])
    odds = rotated(evens, "seq", -1)
    future = jnp.stack([evens, odds], axis=1).reshape(longest, rows, chans)

    lengths, skip, turned, masks = pl.pallas_call(
        stage_kernel,
        out_shape=(
            jax.ShapeDtypeStruct((1, doc_lengths.shape[0]), jnp.int32),
            jax.ShapeDtypeStruct((1, chans), F32),
            jax.ShapeDtypeStruct((chans, rows), BF16),
            jax.ShapeDtypeStruct((evens.shape[0], 8, chans), F32),
        ),
        in_specs=[VMEM] * 3,
        out_specs=(VMEM,) * 4,
        compiler_params=PARAMS,
        name="stage",
    )(doc_lengths.reshape(1, -1), skip_gain.reshape(1, chans), cot_gated)
    owned = maxlag // shards
    grad_scale = 1.0 / math.sqrt(shards * rows * chans * groups)
    parts, sources = pl.pallas_call(
        functools.partial(lag_kernel, owned=owned, copies=groups, scale=grad_scale, shards=shards),
        out_shape=(
            jax.ShapeDtypeStruct((shards * groups, 1, -(-owned // TILE) * TILE), F32),
            jax.ShapeDtypeStruct((2 * rows, chans), BF16),
        ),
        in_specs=[VMEM] * 6,
        out_specs=(VMEM,) * 2,
        compiler_params=PARAMS,
        cost_estimate=pl.CostEstimate(flops=LAGF, bytes_accessed=2**20, transcendentals=0),
        name="lags",
    )(masks, flipped, before, turned, evens, gate_out)
    gathered = lax.all_to_all(parts, ("ch", "seq"), 0, 0, tiled=True)

    band = jax.ShapeDtypeStruct((TILE, maxlag), BF16)
    further = longest // 2 - 1
    later, earlier, ahead = pl.pallas_call(
        ahead_kernel,
        out_shape=(band, band, jax.ShapeDtypeStruct((further, rows, chans), BF16)),
        in_specs=[VMEM] * 3,
        out_specs=(VMEM,) * 3,
        compiler_params=PARAMS,
        name="ahead",
    )(lengths, filter_taps.reshape(1, maxlag), sources)
    far = sum(shifted(ahead[m], "seq", 2 * m + 2).astype(F32) for m in range(further))

    near, grad_value, grad_gate = pl.pallas_call(
        near_kernel,
        out_shape=(jax.ShapeDtypeStruct((rows, chans), F32), block, block),
        in_specs=[VMEM] * 8,
        out_specs=(VMEM,) * 3,
        scratch_shapes=[pltpu.VMEM((maxlag, chans), BF16)],
        compiler_params=PARAMS,
        cost_estimate=pl.CostEstimate(flops=CONVF, bytes_accessed=2**20, transcendentals=0),
        name="near",
    )(lengths, value_proj, gate_in, skip, later, earlier, sources, future)
    layer_out = (gate_out.astype(F32) * (near + far)).astype(BF16)
    filter_grad = pl.pallas_call(
        sum_kernel,
        out_shape=jax.ShapeDtypeStruct((1, owned), F32),
        in_specs=[VMEM, pl.BlockSpec(memory_space=pl.ANY)],
        out_specs=VMEM,
        compiler_params=PARAMS,
        name="sum",
    )(gathered, layer_out)[0]
    return (layer_out, grad_value, grad_gate, filter_grad)


def solution(mesh):
    placed = (P("seq", "ch"), P("seq", "ch"), P("seq", "ch"), P("ch"), P(), P(), P("seq", "ch"))
    return jax.shard_map(
        body,
        mesh=mesh,
        in_specs=placed,
        out_specs=(P("seq", "ch"), P("seq", "ch"), P("seq", "ch"), P("seq")),
        check_vma=False,
    )
```

```python
import functools
import math

import jax
import jax.numpy as jnp
from jax import lax
from jax.experimental import pallas as pl
from jax.experimental.pallas import tpu as pltpu
from jax.sharding import PartitionSpec as P

TILE = 128
LIMIT = 8 * 1024 * 1024
LAGF = 10**10
CONVF = 10**10
F32 = jnp.float32
BF16 = jnp.bfloat16


def shifted(value, axis, by):
    length = lax.axis_size(axis)
    pairs = [(i, i + by) for i in range(length) if 0 <= i + by < length]
    return lax.ppermute(value, axis, pairs)


def rotated(value, axis, by):
    length = lax.axis_size(axis)
    return lax.ppermute(value, axis, [(i, (i + by) % length) for i in range(length)])


def doc_masks(lengths_ref, offsets, chans):
    position = lax.axis_index("seq")
    lengths = lengths_ref[...]
    start = stop = end = jnp.zeros((1, chans), jnp.int32)
    for k in range(lengths.shape[1]):
        begin, end = end, end + jnp.broadcast_to(lengths[:, k : k + 1], end.shape)
        inside = jnp.logical_and(begin <= position, position < end)
        start, stop = jnp.where(inside, begin, start), jnp.where(inside, end, stop)
    masks = []
    for offset in offsets:
        inside = jnp.logical_and(start <= position + offset, position + offset < stop)
        masks.append(jnp.where(inside, 1.0, 0.0).astype(BF16))
    return masks


def flip_matrix():
    row = lax.broadcasted_iota(jnp.int32, (TILE, TILE), 0)
    col = lax.broadcasted_iota(jnp.int32, (TILE, TILE), 1)
    return (row + col == TILE - 1).astype(F32).astype(BF16)


def stage_kernel(lengths_ref, skip_ref, cots_ref, lengths_out_ref, skip_out_ref, turned_ref, masks_ref):
    lengths_out_ref[...] = lengths_ref[...]
    skip_out_ref[...] = skip_ref[...]
    rows, chans = cots_ref.shape
    for at in range(0, rows, TILE):
        turned_ref[:, at : at + TILE] = cots_ref[at : at + TILE, :].astype(F32).T.astype(BF16)
    evens = masks_ref.shape[0]
    for n, mask in enumerate(doc_masks(lengths_ref, [-1] + [2 * e for e in range(1, evens)], chans)):
        masks_ref[n] = jnp.broadcast_to(mask.astype(F32), masks_ref.shape[1:])


def lag_kernel(
    masks_ref, flipped_ref, before_ref, turned_ref, cots_ref, gate_out_ref, parts_ref, sources_ref,
    *, owned, copies, scale, shards,
):
    del gate_out_ref
    evens, rows, chans = cots_ref.shape
    blocks = rows // TILE
    masks = [masks_ref[n, 0:1, :].astype(BF16) for n in range(evens)]
    before = before_ref[...] * masks[0]
    sources = [block[at : at + TILE] for block in (before, flipped_ref[...]) for at in range(0, rows, TILE)]
    zero = jnp.zeros((chans, TILE), BF16)

    def write_parts(used, tiles_before):
        placed = sources[blocks - tiles_before :]
        placed = placed + [jnp.zeros_like(placed[0])] * (len(placed) % 2)
        wide = []
        for e in range(used):
            if e == 0:
                tiles = [turned_ref[:, at : at + TILE] for at in range(0, rows, TILE)]
            else:
                cots = cots_ref[e] * masks[e]
                tiles = [cots[at : at + TILE].astype(F32).T.astype(BF16) for at in range(0, rows, TILE)]
            tiles = [zero] + tiles + [zero]
            wide += [jnp.concatenate(tiles[n : n + 2], axis=0) for n in range(blocks + 1)]
        wide = jnp.concatenate(wide, axis=1)
        sums = [None] * (2 * used * blocks)
        for x in range(0, len(placed), 2):
            source = jnp.concatenate(placed[x : x + 2], axis=1)
            product = jnp.dot(source, wide, preferred_element_type=F32)
            for e in range(used):
                for n in range(blocks + 1):
                    d = 2 * blocks * e + n - 1 + tiles_before - x
                    if d >= 0:
                        at = (e * (blocks + 1) + n) * TILE
                        piece = product[:, at : at + TILE]
                        sums[d] = piece if sums[d] is None else sums[d] + piece
        row = lax.broadcasted_iota(jnp.int32, (TILE, TILE), 0)
        col = lax.broadcasted_iota(jnp.int32, (TILE, TILE), 1)
        sums[0] = jnp.where(row + col >= TILE - 1, sums[0], 0.0)
        sums = [jnp.zeros((TILE, TILE), F32) if piece is None else piece for piece in sums]
        width = len(sums) * TILE
        skewed = pltpu.roll(jnp.concatenate(sums, axis=1), width - TILE + 1, 1, stride=1, stride_axis=0)
        lags = jnp.sum(skewed, axis=0, keepdims=True) * scale
        for p in range(parts_ref.shape[0] // copies):
            some = min(max(width - p * owned, 0), owned)
            pieces = [lags[:, p * owned : p * owned + some]] if some > 0 else []
            pieces += [jnp.zeros((1, owned - some), F32)] if some < owned else []
            piece = pieces[0] if len(pieces) == 1 else jnp.concatenate(pieces, axis=1)
            for q in range(copies):
                parts_ref[q * shards + p, :, :owned] = piece

    if evens == 1:
        write_parts(1, blocks)
    else:
        position = lax.axis_index("seq")
        later = position + 2 < shards
        pl.when(jnp.logical_and(later, position > 0))(functools.partial(write_parts, evens, blocks))
        pl.when(jnp.logical_and(later, position == 0))(functools.partial(write_parts, evens, 0))
        pl.when(jnp.logical_not(later))(functools.partial(write_parts, 1, blocks))
    for n, tile in enumerate(sources[::-1]):
        sources_ref[n * TILE : (n + 1) * TILE, :] = tile


def ahead_kernel(lengths_ref, taps_ref, sources_ref, later_ref, earlier_ref, ahead_ref):
    width = taps_ref.shape[1]
    count = sources_ref.shape[0] // TILE
    further, _, chans = ahead_ref.shape
    masks = doc_masks(lengths_ref, [2 * m for m in range(1, further + 1)], chans)
    rounded = taps_ref[...].astype(BF16).astype(F32)
    skewed = pltpu.roll(jnp.broadcast_to(rounded, (TILE, width)), 0, 1, stride=1, stride_axis=0)
    flip = flip_matrix()
    for d in range(width // TILE):
        block = skewed[:, d * TILE : (d + 1) * TILE]
        if d == 0:
            row = lax.broadcasted_iota(jnp.int32, block.shape, 0)
            col = lax.broadcasted_iota(jnp.int32, block.shape, 1)
            block = jnp.where(col >= row, block, 0.0)
        block = block.astype(BF16)
        later_ref[:, d * TILE : (d + 1) * TILE] = block
        earlier_ref[:, d * TILE : (d + 1) * TILE] = lax.dot_general(
            block, flip, (((0,), (0,)), ((), ())), preferred_element_type=F32
        ).astype(BF16)
    for m in range(1, further + 1):
        for b in range(count // 2):
            first = m * count + b + 1 - count // 2
            part = jnp.dot(
                earlier_ref[:, first * TILE : (first + count) * TILE], sources_ref[...], preferred_element_type=F32
            )
            ahead_ref[m - 1, b * TILE : (b + 1) * TILE, :] = part.astype(BF16) * masks[m - 1]


def near_kernel(
    lengths_ref, value_ref, gate_in_ref, skip_ref, later_ref, earlier_ref, sources_ref, cots_ref,
    near_ref, grad_value_ref, grad_gate_ref, future_ref,
):
    longest, rows, chans = cots_ref.shape
    blocks = rows // TILE
    masks = doc_masks(lengths_ref, range(longest), chans)
    for k in range(longest):
        block = cots_ref[k] if k == 0 else cots_ref[k] * masks[k]
        future_ref[k * rows : (k + 1) * rows, :] = block
    skip = skip_ref[...]
    for b in range(blocks):
        here = slice(b * TILE, (b + 1) * TILE)
        transposed = jnp.dot(
            later_ref[:, : (longest * blocks - b) * TILE], future_ref[b * TILE :, :], preferred_element_type=F32
        )
        through = transposed + skip * cots_ref[0, here, :].astype(F32)
        gate_in, value = gate_in_ref[here, :].astype(F32), value_ref[here, :].astype(F32)
        grad_value_ref[here, :] = (through * gate_in).astype(BF16)
        grad_gate_ref[here, :] = (through * value).astype(BF16)
        newer = blocks - 1 - b
        convolved = jnp.dot(
            earlier_ref[:, : (2 * blocks - newer) * TILE], sources_ref[newer * TILE :, :], preferred_element_type=F32
        )
        near_ref[here, :] = convolved + skip * (gate_in * value).astype(BF16).astype(F32)


def sum_kernel(gathered_ref, layer_out_ref, total_ref):
    del layer_out_ref
    owned = total_ref.shape[1]
    total_ref[...] = jnp.sum(gathered_ref[:, 0, :], axis=0, keepdims=True)[:, :owned]


PARAMS = pltpu.CompilerParams(vmem_limit_bytes=LIMIT)
VMEM = pl.BlockSpec(memory_space=pltpu.VMEM)


def body(value_proj, gate_in, gate_out, skip_gain, filter_taps, doc_lengths, cotangent):
    rows, chans = value_proj.shape
    maxlag = filter_taps.shape[0]
    longest = maxlag // rows
    shards, groups = lax.axis_size("seq"), lax.axis_size("ch")
    block = jax.ShapeDtypeStruct((rows, chans), BF16)
    cot_gated = (cotangent.astype(F32) * gate_out.astype(F32)).astype(BF16)
    gated = (gate_in.astype(F32) * value_proj.astype(F32)).astype(BF16)
    flipped = gated.reshape(rows // TILE, TILE, chans)[:, ::-1].reshape(rows, chans)

    future = cot_gated[None]
    span = longest
    while span > 2:
        span //= 2
        future = jnp.concatenate([future, shifted(future, "seq", -span)], axis=0)
    before = rotated(flipped, "seq", 1)
    bits = max(future.shape[0].bit_length() - 1, 1)
    order = sorted(range(future.shape[0]), key=lambda n: int(format(n, f"0{bits}b")[::-1], 2))
    evens = future if len(order) <= 2 else jnp.stack([future[n] for n in order])
    odds = rotated(evens, "seq", -1)
    future = jnp.stack([evens, odds], axis=1).reshape(longest, rows, chans)

    lengths, skip, turned, masks = pl.pallas_call(
        stage_kernel,
        out_shape=(
            jax.ShapeDtypeStruct((1, doc_lengths.shape[0]), jnp.int32),
            jax.ShapeDtypeStruct((1, chans), F32),
            jax.ShapeDtypeStruct((chans, rows), BF16),
            jax.ShapeDtypeStruct((evens.shape[0], 8, chans), F32),
        ),
        in_specs=[VMEM] * 3,
        out_specs=(VMEM,) * 4,
        compiler_params=PARAMS,
        name="stage",
    )(doc_lengths.reshape(1, -1), skip_gain.reshape(1, chans), cot_gated)
    owned = maxlag // shards
    grad_scale = 1.0 / math.sqrt(shards * rows * chans * groups)
    parts, sources = pl.pallas_call(
        functools.partial(lag_kernel, owned=owned, copies=groups, scale=grad_scale, shards=shards),
        out_shape=(
            jax.ShapeDtypeStruct((shards * groups, 1, -(-owned // TILE) * TILE), F32),
            jax.ShapeDtypeStruct((2 * rows, chans), BF16),
        ),
        in_specs=[VMEM] * 6,
        out_specs=(VMEM,) * 2,
        compiler_params=PARAMS,
        cost_estimate=pl.CostEstimate(flops=LAGF, bytes_accessed=2**20, transcendentals=0),
        name="lags",
    )(masks, flipped, before, turned, evens, gate_out)
    gathered = lax.all_to_all(parts, ("ch", "seq"), 0, 0, tiled=True)

    band = jax.ShapeDtypeStruct((TILE, maxlag), BF16)
    further = longest // 2 - 1
    later, earlier, ahead = pl.pallas_call(
        ahead_kernel,
        out_shape=(band, band, jax.ShapeDtypeStruct((further, rows, chans), BF16)),
        in_specs=[VMEM] * 3,
        out_specs=(VMEM,) * 3,
        compiler_params=PARAMS,
        name="ahead",
    )(lengths, filter_taps.reshape(1, maxlag), sources)
    far = sum(shifted(ahead[m], "seq", 2 * m + 2).astype(F32) for m in range(further))

    near, grad_value, grad_gate = pl.pallas_call(
        near_kernel,
        out_shape=(jax.ShapeDtypeStruct((rows, chans), F32), block, block),
        in_specs=[VMEM] * 8,
        out_specs=(VMEM,) * 3,
        scratch_shapes=[pltpu.VMEM((maxlag, chans), BF16)],
        compiler_params=PARAMS,
        cost_estimate=pl.CostEstimate(flops=CONVF, bytes_accessed=2**20, transcendentals=0),
        name="near",
    )(lengths, value_proj, gate_in, skip, later, earlier, sources, future)
    layer_out = (gate_out.astype(F32) * (near + far)).astype(BF16)
    filter_grad = pl.pallas_call(
        sum_kernel,
        out_shape=jax.ShapeDtypeStruct((1, owned), F32),
        in_specs=[VMEM, pl.BlockSpec(memory_space=pl.ANY)],
        out_specs=VMEM,
        compiler_params=PARAMS,
        name="sum",
    )(gathered, layer_out)[0]
    return (layer_out, grad_value, grad_gate, filter_grad)


def solution(mesh):
    placed = (P("seq", "ch"), P("seq", "ch"), P("seq", "ch"), P("ch"), P(), P(), P("seq", "ch"))
    return jax.shard_map(
        body,
        mesh=mesh,
        in_specs=placed,
        out_specs=(P("seq", "ch"), P("seq", "ch"), P("seq", "ch"), P("seq")),
        check_vma=False,
    )
```

```python
import functools
import math

import jax
import jax.numpy as jnp
from jax import lax
from jax.experimental import pallas as pl
from jax.experimental.pallas import tpu as pltpu
from jax.sharding import PartitionSpec as P

TILE = 128
LIMIT = 8 * 1024 * 1024
LAGF = 10**10
CONVF = 10**10
F32 = jnp.float32
BF16 = jnp.bfloat16


def shifted(value, axis, by):
    length = lax.axis_size(axis)
    pairs = [(i, i + by) for i in range(length) if 0 <= i + by < length]
    return lax.ppermute(value, axis, pairs)


def rotated(value, axis, by):
    length = lax.axis_size(axis)
    return lax.ppermute(value, axis, [(i, (i + by) % length) for i in range(length)])


def doc_masks(lengths_ref, offsets, chans):
    position = lax.axis_index("seq")
    lengths = lengths_ref[...]
    start = stop = end = jnp.zeros((1, chans), jnp.int32)
    for k in range(lengths.shape[1]):
        begin, end = end, end + jnp.broadcast_to(lengths[:, k : k + 1], end.shape)
        inside = jnp.logical_and(begin <= position, position < end)
        start, stop = jnp.where(inside, begin, start), jnp.where(inside, end, stop)
    masks = []
    for offset in offsets:
        inside = jnp.logical_and(start <= position + offset, position + offset < stop)
        masks.append(jnp.where(inside, 1.0, 0.0).astype(BF16))
    return masks


def flip_matrix():
    row = lax.broadcasted_iota(jnp.int32, (TILE, TILE), 0)
    col = lax.broadcasted_iota(jnp.int32, (TILE, TILE), 1)
    return (row + col == TILE - 1).astype(F32).astype(BF16)


def stage_kernel(
    lengths_ref, skip_ref, cots_ref, flipped_ref, lengths_out_ref, skip_out_ref, turned_ref, masks_ref, own_ref, picks_ref,
    *, owned, starts,
):
    lengths_out_ref[...] = lengths_ref[...]
    skip_out_ref[...] = skip_ref[...]
    rows, chans = cots_ref.shape
    for at in range(0, rows, TILE):
        turned_ref[:, at : at + TILE] = cots_ref[at : at + TILE, :].astype(F32).T.astype(BF16)
    skipped = lax.axis_index("seq") * owned % TILE
    for n, start in enumerate(starts):
        picks_ref[n] = jnp.full(picks_ref.shape[1:], (skipped == start).astype(F32))
    own = [None] * (rows // TILE)
    for sb in range(len(own)):
        product = jnp.dot(
            flipped_ref[sb * TILE : (sb + 1) * TILE, :], turned_ref[:, sb * TILE :], preferred_element_type=F32
        )
        for d in range(len(own) - sb):
            piece = product[:, d * TILE : (d + 1) * TILE]
            own[d] = piece if own[d] is None else own[d] + piece
    for d, piece in enumerate(own):
        own_ref[:, d * TILE : (d + 1) * TILE] = piece
    evens = masks_ref.shape[0]
    for n, mask in enumerate(doc_masks(lengths_ref, [-1] + [2 * e for e in range(1, evens)], chans)):
        masks_ref[n] = jnp.broadcast_to(mask.astype(F32), masks_ref.shape[1:])


def lag_kernel(
    masks_ref, flipped_ref, before_ref, turned_ref, own_ref, cots_ref, gate_out_ref, parts_ref, sources_ref,
    *, owned, copies, scale, shards,
):
    del gate_out_ref
    evens, rows, chans = cots_ref.shape
    blocks = rows // TILE
    masks = [masks_ref[n, 0:1, :].astype(BF16) for n in range(evens)]
    before = before_ref[...] * masks[0]
    sources = [block[at : at + TILE] for block in (before, flipped_ref[...]) for at in range(0, rows, TILE)]
    zero = jnp.zeros((chans, TILE), BF16)

    def write_parts(used, tiles_before):
        sums = [own_ref[:, d * TILE : (d + 1) * TILE] if d < blocks else None for d in range(2 * used * blocks)]
        for e in range(used):
            placed = sources[blocks - tiles_before :]
            if e == 0:
                placed = placed[:tiles_before]
                tiles = [turned_ref[:, at : at + TILE] for at in range(0, rows, TILE)]
            else:
                cots = cots_ref[e] * masks[e]
                tiles = [cots[at : at + TILE].astype(F32).T.astype(BF16) for at in range(0, rows, TILE)]
            placed = placed + [jnp.zeros((TILE, chans), BF16)] * (len(placed) % 2)
            tiles = [zero] + tiles + [zero]
            wide = jnp.concatenate([jnp.concatenate(tiles[n : n + 2], axis=0) for n in range(blocks + 1)], axis=1)
            for x in range(0, len(placed), 2):
                source = jnp.concatenate(placed[x : x + 2], axis=1)
                product = jnp.dot(source, wide, preferred_element_type=F32)
                for n in range(blocks + 1):
                    d = 2 * blocks * e + n - 1 + tiles_before - x
                    if d >= 0:
                        piece = product[:, n * TILE : (n + 1) * TILE]
                        sums[d] = piece if sums[d] is None else sums[d] + piece
        row = lax.broadcasted_iota(jnp.int32, (TILE, TILE), 0)
        col = lax.broadcasted_iota(jnp.int32, (TILE, TILE), 1)
        sums[0] = jnp.where(row + col >= TILE - 1, sums[0], 0.0)
        sums = [jnp.zeros((TILE, TILE), F32) if piece is None else piece for piece in sums]
        width = len(sums) * TILE
        skewed = pltpu.roll(jnp.concatenate(sums, axis=1), width - TILE + 1, 1, stride=1, stride_axis=0)
        lags = jnp.sum(skewed, axis=0, keepdims=True) * scale
        window = parts_ref.shape[2]
        for p in range(parts_ref.shape[0] // copies):
            first = p * owned // TILE * TILE
            last = min(first + window, width)
            for q in range(copies):
                if first < last:
                    parts_ref[q * shards + p, :, : last - first] = lags[:, first:last]
                if last < first + window:
                    rest = max(last - first, 0)
                    parts_ref[q * shards + p, :, rest:] = jnp.zeros((1, window - rest), F32)

    if evens == 1:
        write_parts(1, blocks)
    else:
        position = lax.axis_index("seq")
        later = position + 2 < shards
        pl.when(jnp.logical_and(later, position > 0))(functools.partial(write_parts, evens, blocks))
        pl.when(jnp.logical_and(later, position == 0))(functools.partial(write_parts, evens, 0))
        pl.when(jnp.logical_not(later))(functools.partial(write_parts, 1, blocks))
    for n, tile in enumerate(sources[::-1]):
        sources_ref[n * TILE : (n + 1) * TILE, :] = tile


def ahead_kernel(lengths_ref, taps_ref, sources_ref, later_ref, earlier_ref, ahead_ref):
    width = taps_ref.shape[1]
    count = sources_ref.shape[0] // TILE
    further, _, chans = ahead_ref.shape
    masks = doc_masks(lengths_ref, [2 * m for m in range(1, further + 1)], chans)
    rounded = taps_ref[...].astype(BF16).astype(F32)
    skewed = pltpu.roll(jnp.broadcast_to(rounded, (TILE, width)), 0, 1, stride=1, stride_axis=0)
    flip = flip_matrix()
    for d in range(width // TILE):
        block = skewed[:, d * TILE : (d + 1) * TILE]
        if d == 0:
            row = lax.broadcasted_iota(jnp.int32, block.shape, 0)
            col = lax.broadcasted_iota(jnp.int32, block.shape, 1)
            block = jnp.where(col >= row, block, 0.0)
        block = block.astype(BF16)
        later_ref[:, d * TILE : (d + 1) * TILE] = block
        earlier_ref[:, d * TILE : (d + 1) * TILE] = lax.dot_general(
            block, flip, (((0,), (0,)), ((), ())), preferred_element_type=F32
        ).astype(BF16)
    for m in range(1, further + 1):
        for b in range(count // 2):
            first = m * count + b + 1 - count // 2
            part = jnp.dot(
                earlier_ref[:, first * TILE : (first + count) * TILE], sources_ref[...], preferred_element_type=F32
            )
            ahead_ref[m - 1, b * TILE : (b + 1) * TILE, :] = part.astype(BF16) * masks[m - 1]


def near_kernel(
    lengths_ref, value_ref, gate_in_ref, skip_ref, later_ref, earlier_ref, sources_ref, cots_ref,
    near_ref, grad_value_ref, grad_gate_ref, future_ref,
):
    longest, rows, chans = cots_ref.shape
    blocks = rows // TILE
    masks = doc_masks(lengths_ref, range(longest), chans)
    for k in range(longest):
        block = cots_ref[k] if k == 0 else cots_ref[k] * masks[k]
        future_ref[k * rows : (k + 1) * rows, :] = block
    skip = skip_ref[...]
    for b in range(blocks):
        here = slice(b * TILE, (b + 1) * TILE)
        transposed = jnp.dot(
            later_ref[:, : (longest * blocks - b) * TILE], future_ref[b * TILE :, :], preferred_element_type=F32
        )
        through = transposed + skip * cots_ref[0, here, :].astype(F32)
        gate_in, value = gate_in_ref[here, :].astype(F32), value_ref[here, :].astype(F32)
        grad_value_ref[here, :] = (through * gate_in).astype(BF16)
        grad_gate_ref[here, :] = (through * value).astype(BF16)
        newer = blocks - 1 - b
        convolved = jnp.dot(
            earlier_ref[:, : (2 * blocks - newer) * TILE], sources_ref[newer * TILE :, :], preferred_element_type=F32
        )
        near_ref[here, :] = convolved + skip * (gate_in * value).astype(BF16).astype(F32)


def sum_kernel(gathered_ref, picks_ref, layer_out_ref, total_ref, *, starts):
    del layer_out_ref
    owned = total_ref.shape[1]
    total = jnp.sum(gathered_ref[:, 0, :], axis=0, keepdims=True)
    owner = total[:, : owned]
    for n, start in enumerate(starts):
        if start > 0:
            owner = jnp.where(picks_ref[n, 0:1, :owned] > 0.0, total[:, start : start + owned], owner)
    total_ref[...] = owner


PARAMS = pltpu.CompilerParams(vmem_limit_bytes=LIMIT)
VMEM = pl.BlockSpec(memory_space=pltpu.VMEM)


def body(value_proj, gate_in, gate_out, skip_gain, filter_taps, doc_lengths, cotangent):
    rows, chans = value_proj.shape
    maxlag = filter_taps.shape[0]
    longest = maxlag // rows
    shards, groups = lax.axis_size("seq"), lax.axis_size("ch")
    block = jax.ShapeDtypeStruct((rows, chans), BF16)
    cot_gated = (cotangent.astype(F32) * gate_out.astype(F32)).astype(BF16)
    gated = (gate_in.astype(F32) * value_proj.astype(F32)).astype(BF16)
    flipped = gated.reshape(rows // TILE, TILE, chans)[:, ::-1].reshape(rows, chans)

    future = cot_gated[None]
    span = longest
    while span > 2:
        span //= 2
        future = jnp.concatenate([future, shifted(future, "seq", -span)], axis=0)
    before = rotated(flipped, "seq", 1)
    bits = max(future.shape[0].bit_length() - 1, 1)
    order = sorted(range(future.shape[0]), key=lambda n: int(format(n, f"0{bits}b")[::-1], 2))
    evens = future if len(order) <= 2 else jnp.stack([future[n] for n in order])
    odds = rotated(evens, "seq", -1)
    future = jnp.stack([evens, odds], axis=1).reshape(longest, rows, chans)

    owned = maxlag // shards
    starts = tuple(sorted({p * owned % TILE for p in range(shards)}))
    window = -(-(starts[-1] + owned) // TILE) * TILE
    lengths, skip, turned, masks, own, picks = pl.pallas_call(
        functools.partial(stage_kernel, owned=owned, starts=starts),
        out_shape=(
            jax.ShapeDtypeStruct((1, doc_lengths.shape[0]), jnp.int32),
            jax.ShapeDtypeStruct((1, chans), F32),
            jax.ShapeDtypeStruct((chans, rows), BF16),
            jax.ShapeDtypeStruct((evens.shape[0], 8, chans), F32),
            jax.ShapeDtypeStruct((TILE, rows), F32),
            jax.ShapeDtypeStruct((len(starts), 8, window), F32),
        ),
        in_specs=[VMEM] * 4,
        out_specs=(VMEM,) * 6,
        compiler_params=PARAMS,
        name="stage",
    )(doc_lengths.reshape(1, -1), skip_gain.reshape(1, chans), cot_gated, flipped)
    grad_scale = 1.0 / math.sqrt(shards * rows * chans * groups)
    parts, sources = pl.pallas_call(
        functools.partial(lag_kernel, owned=owned, copies=groups, scale=grad_scale, shards=shards),
        out_shape=(
            jax.ShapeDtypeStruct((shards * groups, 1, window), F32),
            jax.ShapeDtypeStruct((2 * rows, chans), BF16),
        ),
        in_specs=[VMEM] * 7,
        out_specs=(VMEM,) * 2,
        compiler_params=PARAMS,
        cost_estimate=pl.CostEstimate(flops=LAGF, bytes_accessed=2**20, transcendentals=0),
        name="lags",
    )(masks, flipped, before, turned, own, evens, gate_out)
    gathered = lax.all_to_all(parts, ("ch", "seq"), 0, 0, tiled=True)

    band = jax.ShapeDtypeStruct((TILE, maxlag), BF16)
    further = longest // 2 - 1
    later, earlier, ahead = pl.pallas_call(
        ahead_kernel,
        out_shape=(band, band, jax.ShapeDtypeStruct((further, rows, chans), BF16)),
        in_specs=[VMEM] * 3,
        out_specs=(VMEM,) * 3,
        compiler_params=PARAMS,
        name="ahead",
    )(lengths, filter_taps.reshape(1, maxlag), sources)
    far = sum(shifted(ahead[m], "seq", 2 * m + 2).astype(F32) for m in range(further))

    near, grad_value, grad_gate = pl.pallas_call(
        near_kernel,
        out_shape=(jax.ShapeDtypeStruct((rows, chans), F32), block, block),
        in_specs=[VMEM] * 8,
        out_specs=(VMEM,) * 3,
        scratch_shapes=[pltpu.VMEM((maxlag, chans), BF16)],
        compiler_params=PARAMS,
        cost_estimate=pl.CostEstimate(flops=CONVF, bytes_accessed=2**20, transcendentals=0),
        name="near",
    )(lengths, value_proj, gate_in, skip, later, earlier, sources, future)
    layer_out = (gate_out.astype(F32) * (near + far)).astype(BF16)
    filter_grad = pl.pallas_call(
        functools.partial(sum_kernel, starts=starts),
        out_shape=jax.ShapeDtypeStruct((1, owned), F32),
        in_specs=[VMEM, VMEM, pl.BlockSpec(memory_space=pl.ANY)],
        out_specs=VMEM,
        compiler_params=PARAMS,
        name="sum",
    )(gathered, picks, layer_out)[0]
    return (layer_out, grad_value, grad_gate, filter_grad)


def solution(mesh):
    placed = (P("seq", "ch"), P("seq", "ch"), P("seq", "ch"), P("ch"), P(), P(), P("seq", "ch"))
    return jax.shard_map(
        body,
        mesh=mesh,
        in_specs=placed,
        out_specs=(P("seq", "ch"), P("seq", "ch"), P("seq", "ch"), P("seq")),
        check_vma=False,
    )
```

```python
import functools
import math

import jax
import jax.numpy as jnp
from jax import lax
from jax.experimental import pallas as pl
from jax.experimental.pallas import tpu as pltpu
from jax.sharding import PartitionSpec as P

TILE = 128
LIMIT = 8 * 1024 * 1024
LAGF = 10**10
CONVF = 10**10
F32 = jnp.float32
BF16 = jnp.bfloat16


def shifted(value, axis, by):
    length = lax.axis_size(axis)
    pairs = [(i, i + by) for i in range(length) if 0 <= i + by < length]
    return lax.ppermute(value, axis, pairs)


def rotated(value, axis, by):
    length = lax.axis_size(axis)
    return lax.ppermute(value, axis, [(i, (i + by) % length) for i in range(length)])


def doc_masks(lengths_ref, offsets, chans):
    position = lax.axis_index("seq")
    lengths = lengths_ref[...]
    start = stop = end = jnp.zeros((1, chans), jnp.int32)
    for k in range(lengths.shape[1]):
        begin, end = end, end + jnp.broadcast_to(lengths[:, k : k + 1], end.shape)
        inside = jnp.logical_and(begin <= position, position < end)
        start, stop = jnp.where(inside, begin, start), jnp.where(inside, end, stop)
    masks = []
    for offset in offsets:
        inside = jnp.logical_and(start <= position + offset, position + offset < stop)
        masks.append(jnp.where(inside, 1.0, 0.0).astype(BF16))
    return masks


def flip_matrix():
    row = lax.broadcasted_iota(jnp.int32, (TILE, TILE), 0)
    col = lax.broadcasted_iota(jnp.int32, (TILE, TILE), 1)
    return (row + col == TILE - 1).astype(F32).astype(BF16)


def stage_kernel(
    lengths_ref, skip_ref, cots_ref, flipped_ref, lengths_out_ref, skip_out_ref, turned_ref, masks_ref, own_ref, picks_ref,
    *, owned, starts,
):
    lengths_out_ref[...] = lengths_ref[...]
    skip_out_ref[...] = skip_ref[...]
    rows, chans = cots_ref.shape
    for at in range(0, rows, TILE):
        turned_ref[:, at : at + TILE] = cots_ref[at : at + TILE, :].astype(F32).T.astype(BF16)
    skipped = lax.axis_index("seq") * owned % TILE
    for n, start in enumerate(starts):
        picks_ref[n] = jnp.full(picks_ref.shape[1:], (skipped == start).astype(F32))
    own = [None] * (rows // TILE)
    for sb in range(len(own)):
        product = jnp.dot(
            flipped_ref[sb * TILE : (sb + 1) * TILE, :], turned_ref[:, sb * TILE :], preferred_element_type=F32
        )
        for d in range(len(own) - sb):
            piece = product[:, d * TILE : (d + 1) * TILE]
            own[d] = piece if own[d] is None else own[d] + piece
    for d, piece in enumerate(own):
        own_ref[:, d * TILE : (d + 1) * TILE] = piece
    evens = masks_ref.shape[0]
    for n, mask in enumerate(doc_masks(lengths_ref, [-1] + [2 * e for e in range(1, evens)], chans)):
        masks_ref[n] = jnp.broadcast_to(mask.astype(F32), masks_ref.shape[1:])


def lag_kernel(
    masks_ref, flipped_ref, before_ref, turned_ref, own_ref, cots_ref, gate_out_ref, parts_ref,
    *, owned, copies, scale, shards,
):
    del gate_out_ref
    evens, rows, chans = cots_ref.shape
    blocks = rows // TILE
    masks = [masks_ref[n, 0:1, :].astype(BF16) for n in range(evens)]
    before = before_ref[...] * masks[0]
    sources = [block[at : at + TILE] for block in (before, flipped_ref[...]) for at in range(0, rows, TILE)]
    zero = jnp.zeros((chans, TILE), BF16)

    def write_parts(used, tiles_before):
        sums = [own_ref[:, d * TILE : (d + 1) * TILE] if d < blocks else None for d in range(2 * used * blocks)]
        for e in range(used):
            placed = sources[blocks - tiles_before :]
            if e == 0:
                placed = placed[:tiles_before]
                tiles = [turned_ref[:, at : at + TILE] for at in range(0, rows, TILE)]
            else:
                cots = cots_ref[e] * masks[e]
                tiles = [cots[at : at + TILE].astype(F32).T.astype(BF16) for at in range(0, rows, TILE)]
            placed = placed + [jnp.zeros((TILE, chans), BF16)] * (len(placed) % 2)
            tiles = [zero] + tiles + [zero]
            wide = jnp.concatenate([jnp.concatenate(tiles[n : n + 2], axis=0) for n in range(blocks + 1)], axis=1)
            for x in range(0, len(placed), 2):
                source = jnp.concatenate(placed[x : x + 2], axis=1)
                product = jnp.dot(source, wide, preferred_element_type=F32)
                for n in range(blocks + 1):
                    d = 2 * blocks * e + n - 1 + tiles_before - x
                    if d >= 0:
                        piece = product[:, n * TILE : (n + 1) * TILE]
                        sums[d] = piece if sums[d] is None else sums[d] + piece
        row = lax.broadcasted_iota(jnp.int32, (TILE, TILE), 0)
        col = lax.broadcasted_iota(jnp.int32, (TILE, TILE), 1)
        sums[0] = jnp.where(row + col >= TILE - 1, sums[0], 0.0)
        sums = [jnp.zeros((TILE, TILE), F32) if piece is None else piece for piece in sums]
        width = len(sums) * TILE
        skewed = pltpu.roll(jnp.concatenate(sums, axis=1), width - TILE + 1, 1, stride=1, stride_axis=0)
        lags = jnp.sum(skewed, axis=0, keepdims=True) * scale
        window = parts_ref.shape[2]
        for p in range(parts_ref.shape[0] // copies):
            first = p * owned // TILE * TILE
            last = min(first + window, width)
            for q in range(copies):
                if first < last:
                    parts_ref[q * shards + p, :, : last - first] = lags[:, first:last]
                if last < first + window:
                    rest = max(last - first, 0)
                    parts_ref[q * shards + p, :, rest:] = jnp.zeros((1, window - rest), F32)

    if evens == 1:
        write_parts(1, blocks)
    else:
        position = lax.axis_index("seq")
        later = position + 2 < shards
        pl.when(jnp.logical_and(later, position > 0))(functools.partial(write_parts, evens, blocks))
        pl.when(jnp.logical_and(later, position == 0))(functools.partial(write_parts, evens, 0))
        pl.when(jnp.logical_not(later))(functools.partial(write_parts, 1, blocks))


def ahead_kernel(
    lengths_ref, taps_ref, masks_ref, flipped_ref, before_ref, parts_ref,
    later_ref, earlier_ref, ahead_ref, sources_ref,
):
    del parts_ref
    tiles = sources_ref.shape[0] // TILE // 2
    before = before_ref[...] * masks_ref[0, 0:1, :].astype(BF16)
    for b in range(tiles):
        sources_ref[(tiles - 1 - b) * TILE : (tiles - b) * TILE, :] = flipped_ref[b * TILE : (b + 1) * TILE, :]
        sources_ref[(2 * tiles - 1 - b) * TILE : (2 * tiles - b) * TILE, :] = before[b * TILE : (b + 1) * TILE]
    width = taps_ref.shape[1]
    count = sources_ref.shape[0] // TILE
    further, _, chans = ahead_ref.shape
    masks = doc_masks(lengths_ref, [2 * m for m in range(1, further + 1)], chans)
    rounded = taps_ref[...].astype(BF16).astype(F32)
    skewed = pltpu.roll(jnp.broadcast_to(rounded, (TILE, width)), 0, 1, stride=1, stride_axis=0)
    flip = flip_matrix()
    for d in range(width // TILE):
        block = skewed[:, d * TILE : (d + 1) * TILE]
        if d == 0:
            row = lax.broadcasted_iota(jnp.int32, block.shape, 0)
            col = lax.broadcasted_iota(jnp.int32, block.shape, 1)
            block = jnp.where(col >= row, block, 0.0)
        block = block.astype(BF16)
        later_ref[:, d * TILE : (d + 1) * TILE] = block
        earlier_ref[:, d * TILE : (d + 1) * TILE] = lax.dot_general(
            block, flip, (((0,), (0,)), ((), ())), preferred_element_type=F32
        ).astype(BF16)
    for m in range(1, further + 1):
        for b in range(count // 2):
            first = m * count + b + 1 - count // 2
            part = jnp.dot(
                earlier_ref[:, first * TILE : (first + count) * TILE], sources_ref[...], preferred_element_type=F32
            )
            ahead_ref[m - 1, b * TILE : (b + 1) * TILE, :] = part.astype(BF16) * masks[m - 1]


def near_kernel(
    lengths_ref, value_ref, gate_in_ref, skip_ref, later_ref, earlier_ref, sources_ref, cots_ref,
    near_ref, grad_value_ref, grad_gate_ref, future_ref,
):
    longest, rows, chans = cots_ref.shape
    blocks = rows // TILE
    masks = doc_masks(lengths_ref, range(longest), chans)
    for k in range(longest):
        block = cots_ref[k] if k == 0 else cots_ref[k] * masks[k]
        future_ref[k * rows : (k + 1) * rows, :] = block
    skip = skip_ref[...]
    for b in range(blocks):
        here = slice(b * TILE, (b + 1) * TILE)
        transposed = jnp.dot(
            later_ref[:, : (longest * blocks - b) * TILE], future_ref[b * TILE :, :], preferred_element_type=F32
        )
        through = transposed + skip * cots_ref[0, here, :].astype(F32)
        gate_in, value = gate_in_ref[here, :].astype(F32), value_ref[here, :].astype(F32)
        grad_value_ref[here, :] = (through * gate_in).astype(BF16)
        grad_gate_ref[here, :] = (through * value).astype(BF16)
        newer = blocks - 1 - b
        convolved = jnp.dot(
            earlier_ref[:, : (2 * blocks - newer) * TILE], sources_ref[newer * TILE :, :], preferred_element_type=F32
        )
        near_ref[here, :] = convolved + skip * (gate_in * value).astype(BF16).astype(F32)


def sum_kernel(gathered_ref, picks_ref, layer_out_ref, total_ref, *, starts):
    del layer_out_ref
    owned = total_ref.shape[1]
    total = jnp.sum(gathered_ref[:, 0, :], axis=0, keepdims=True)
    owner = total[:, : owned]
    for n, start in enumerate(starts):
        if start > 0:
            owner = jnp.where(picks_ref[n, 0:1, :owned] > 0.0, total[:, start : start + owned], owner)
    total_ref[...] = owner


PARAMS = pltpu.CompilerParams(vmem_limit_bytes=LIMIT)
VMEM = pl.BlockSpec(memory_space=pltpu.VMEM)


def body(value_proj, gate_in, gate_out, skip_gain, filter_taps, doc_lengths, cotangent):
    rows, chans = value_proj.shape
    maxlag = filter_taps.shape[0]
    longest = maxlag // rows
    shards, groups = lax.axis_size("seq"), lax.axis_size("ch")
    block = jax.ShapeDtypeStruct((rows, chans), BF16)
    cot_gated = (cotangent.astype(F32) * gate_out.astype(F32)).astype(BF16)
    gated = (gate_in.astype(F32) * value_proj.astype(F32)).astype(BF16)
    flipped = gated.reshape(rows // TILE, TILE, chans)[:, ::-1].reshape(rows, chans)

    future = cot_gated[None]
    span = longest
    while span > 2:
        span //= 2
        future = jnp.concatenate([future, shifted(future, "seq", -span)], axis=0)
    before = rotated(flipped, "seq", 1)
    bits = max(future.shape[0].bit_length() - 1, 1)
    order = sorted(range(future.shape[0]), key=lambda n: int(format(n, f"0{bits}b")[::-1], 2))
    evens = future if len(order) <= 2 else jnp.stack([future[n] for n in order])
    odds = rotated(evens, "seq", -1)
    future = jnp.stack([evens, odds], axis=1).reshape(longest, rows, chans)

    owned = maxlag // shards
    starts = tuple(sorted({p * owned % TILE for p in range(shards)}))
    window = -(-(starts[-1] + owned) // TILE) * TILE
    lengths, skip, turned, masks, own, picks = pl.pallas_call(
        functools.partial(stage_kernel, owned=owned, starts=starts),
        out_shape=(
            jax.ShapeDtypeStruct((1, doc_lengths.shape[0]), jnp.int32),
            jax.ShapeDtypeStruct((1, chans), F32),
            jax.ShapeDtypeStruct((chans, rows), BF16),
            jax.ShapeDtypeStruct((evens.shape[0], 8, chans), F32),
            jax.ShapeDtypeStruct((TILE, rows), F32),
            jax.ShapeDtypeStruct((len(starts), 8, window), F32),
        ),
        in_specs=[VMEM] * 4,
        out_specs=(VMEM,) * 6,
        compiler_params=PARAMS,
        name="stage",
    )(doc_lengths.reshape(1, -1), skip_gain.reshape(1, chans), cot_gated, flipped)
    grad_scale = 1.0 / math.sqrt(shards * rows * chans * groups)
    parts = pl.pallas_call(
        functools.partial(lag_kernel, owned=owned, copies=groups, scale=grad_scale, shards=shards),
        out_shape=jax.ShapeDtypeStruct((shards * groups, 1, window), F32),
        in_specs=[VMEM] * 7,
        out_specs=VMEM,
        compiler_params=PARAMS,
        cost_estimate=pl.CostEstimate(flops=LAGF, bytes_accessed=2**20, transcendentals=0),
        name="lags",
    )(masks, flipped, before, turned, own, evens, gate_out)
    gathered = lax.all_to_all(parts, ("ch", "seq"), 0, 0, tiled=True)

    band = jax.ShapeDtypeStruct((TILE, maxlag), BF16)
    further = longest // 2 - 1
    later, earlier, ahead, sources = pl.pallas_call(
        ahead_kernel,
        out_shape=(
            band, band, jax.ShapeDtypeStruct((further, rows, chans), BF16), jax.ShapeDtypeStruct((2 * rows, chans), BF16)
        ),
        in_specs=[VMEM] * 5 + [pl.BlockSpec(memory_space=pl.ANY)],
        out_specs=(VMEM,) * 4,
        compiler_params=PARAMS,
        name="ahead",
    )(lengths, filter_taps.reshape(1, maxlag), masks, flipped, before, parts)
    far = sum(shifted(ahead[m], "seq", 2 * m + 2).astype(F32) for m in range(further))

    near, grad_value, grad_gate = pl.pallas_call(
        near_kernel,
        out_shape=(jax.ShapeDtypeStruct((rows, chans), F32), block, block),
        in_specs=[VMEM] * 8,
        out_specs=(VMEM,) * 3,
        scratch_shapes=[pltpu.VMEM((maxlag, chans), BF16)],
        compiler_params=PARAMS,
        cost_estimate=pl.CostEstimate(flops=CONVF, bytes_accessed=2**20, transcendentals=0),
        name="near",
    )(lengths, value_proj, gate_in, skip, later, earlier, sources, future)
    layer_out = (gate_out.astype(F32) * (near + far)).astype(BF16)
    filter_grad = pl.pallas_call(
        functools.partial(sum_kernel, starts=starts),
        out_shape=jax.ShapeDtypeStruct((1, owned), F32),
        in_specs=[VMEM, VMEM, pl.BlockSpec(memory_space=pl.ANY)],
        out_specs=VMEM,
        compiler_params=PARAMS,
        name="sum",
    )(gathered, picks, layer_out)[0]
    return (layer_out, grad_value, grad_gate, filter_grad)


def solution(mesh):
    placed = (P("seq", "ch"), P("seq", "ch"), P("seq", "ch"), P("ch"), P(), P(), P("seq", "ch"))
    return jax.shard_map(
        body,
        mesh=mesh,
        in_specs=placed,
        out_specs=(P("seq", "ch"), P("seq", "ch"), P("seq", "ch"), P("seq")),
        check_vma=False,
    )
```

```python
import functools
import math

import jax
import jax.numpy as jnp
from jax import lax
from jax.experimental import pallas as pl
from jax.experimental.pallas import tpu as pltpu
from jax.sharding import PartitionSpec as P

TILE = 128
LIMIT = 8 * 1024 * 1024
LAGF = 10**10
CONVF = 10**10
F32 = jnp.float32
BF16 = jnp.bfloat16


def shifted(value, axis, by):
    length = lax.axis_size(axis)
    pairs = [(i, i + by) for i in range(length) if 0 <= i + by < length]
    return lax.ppermute(value, axis, pairs)


def rotated(value, axis, by):
    length = lax.axis_size(axis)
    return lax.ppermute(value, axis, [(i, (i + by) % length) for i in range(length)])


def doc_masks(lengths_ref, offsets, chans):
    position = lax.axis_index("seq")
    lengths = lengths_ref[...]
    start = stop = end = jnp.zeros((1, chans), jnp.int32)
    for k in range(lengths.shape[1]):
        begin, end = end, end + jnp.broadcast_to(lengths[:, k : k + 1], end.shape)
        inside = jnp.logical_and(begin <= position, position < end)
        start, stop = jnp.where(inside, begin, start), jnp.where(inside, end, stop)
    masks = []
    for offset in offsets:
        inside = jnp.logical_and(start <= position + offset, position + offset < stop)
        masks.append(jnp.where(inside, 1.0, 0.0).astype(BF16))
    return masks


def flip_matrix():
    row = lax.broadcasted_iota(jnp.int32, (TILE, TILE), 0)
    col = lax.broadcasted_iota(jnp.int32, (TILE, TILE), 1)
    return (row + col == TILE - 1).astype(F32).astype(BF16)


def stage_kernel(
    lengths_ref, skip_ref, cots_ref, flipped_ref, lengths_out_ref, skip_out_ref, turned_ref, masks_ref, own_ref, picks_ref,
    *, owned, starts,
):
    lengths_out_ref[...] = lengths_ref[...]
    skip_out_ref[...] = skip_ref[...]
    rows, chans = cots_ref.shape
    for at in range(0, rows, TILE):
        turned_ref[:, at : at + TILE] = cots_ref[at : at + TILE, :].astype(F32).T.astype(BF16)
    skipped = lax.axis_index("seq") * owned % TILE
    for n, start in enumerate(starts):
        picks_ref[n] = jnp.full(picks_ref.shape[1:], (skipped == start).astype(F32))
    own = [None] * (rows // TILE)
    for sb in range(len(own)):
        product = jnp.dot(
            flipped_ref[sb * TILE : (sb + 1) * TILE, :], turned_ref[:, sb * TILE :], preferred_element_type=F32
        )
        for d in range(len(own) - sb):
            piece = product[:, d * TILE : (d + 1) * TILE]
            own[d] = piece if own[d] is None else own[d] + piece
    for d, piece in enumerate(own):
        own_ref[:, d * TILE : (d + 1) * TILE] = piece
    evens = masks_ref.shape[0]
    for n, mask in enumerate(doc_masks(lengths_ref, [-1] + [2 * e for e in range(1, evens)], chans)):
        masks_ref[n] = jnp.broadcast_to(mask.astype(F32), masks_ref.shape[1:])


def lag_kernel(
    masks_ref, flipped_ref, before_ref, turned_ref, own_ref, cots_ref, gate_out_ref, parts_ref,
    *, owned, copies, shards,
):
    del gate_out_ref
    evens, rows, chans = cots_ref.shape
    blocks = rows // TILE
    masks = [masks_ref[n, 0:1, :].astype(BF16) for n in range(evens)]
    before = before_ref[...] * masks[0]
    sources = [block[at : at + TILE] for block in (before, flipped_ref[...]) for at in range(0, rows, TILE)]
    zero = jnp.zeros((chans, TILE), BF16)

    def write_parts(used, tiles_before):
        sums = [own_ref[:, d * TILE : (d + 1) * TILE] if d < blocks else None for d in range(2 * used * blocks)]
        for e in range(used):
            placed = sources[blocks - tiles_before :]
            if e == 0:
                placed = placed[:tiles_before]
                tiles = [turned_ref[:, at : at + TILE] for at in range(0, rows, TILE)]
            else:
                cots = cots_ref[e] * masks[e]
                tiles = [cots[at : at + TILE].astype(F32).T.astype(BF16) for at in range(0, rows, TILE)]
            placed = placed + [jnp.zeros((TILE, chans), BF16)] * (len(placed) % 2)
            tiles = [zero] + tiles + [zero]
            wide = jnp.concatenate([jnp.concatenate(tiles[n : n + 2], axis=0) for n in range(blocks + 1)], axis=1)
            for x in range(0, len(placed), 2):
                source = jnp.concatenate(placed[x : x + 2], axis=1)
                product = jnp.dot(source, wide, preferred_element_type=F32)
                for n in range(blocks + 1):
                    d = 2 * blocks * e + n - 1 + tiles_before - x
                    if d >= 0:
                        piece = product[:, n * TILE : (n + 1) * TILE]
                        sums[d] = piece if sums[d] is None else sums[d] + piece
        row = lax.broadcasted_iota(jnp.int32, (TILE, TILE), 0)
        col = lax.broadcasted_iota(jnp.int32, (TILE, TILE), 1)
        sums[0] = jnp.where(row + col >= TILE - 1, sums[0], 0.0)
        sums = [jnp.zeros((TILE, TILE), F32) if piece is None else piece for piece in sums]
        width = len(sums) * TILE
        skewed = pltpu.roll(jnp.concatenate(sums, axis=1), width - TILE + 1, 1, stride=1, stride_axis=0)
        lags = jnp.sum(skewed, axis=0, keepdims=True)
        window = parts_ref.shape[2]
        for p in range(parts_ref.shape[0] // copies):
            first = p * owned // TILE * TILE
            last = min(first + window, width)
            for q in range(copies):
                if first < last:
                    parts_ref[q * shards + p, :, : last - first] = lags[:, first:last]
                if last < first + window:
                    rest = max(last - first, 0)
                    parts_ref[q * shards + p, :, rest:] = jnp.zeros((1, window - rest), F32)

    if evens == 1:
        write_parts(1, blocks)
    else:
        position = lax.axis_index("seq")
        later = position + 2 < shards
        pl.when(jnp.logical_and(later, position > 0))(functools.partial(write_parts, evens, blocks))
        pl.when(jnp.logical_and(later, position == 0))(functools.partial(write_parts, evens, 0))
        pl.when(jnp.logical_not(later))(functools.partial(write_parts, 1, blocks))


def ahead_kernel(
    lengths_ref, taps_ref, masks_ref, flipped_ref, before_ref, parts_ref,
    later_ref, earlier_ref, ahead_ref, sources_ref,
):
    del parts_ref
    tiles = sources_ref.shape[0] // TILE // 2
    before = before_ref[...] * masks_ref[0, 0:1, :].astype(BF16)
    for b in range(tiles):
        sources_ref[(tiles - 1 - b) * TILE : (tiles - b) * TILE, :] = flipped_ref[b * TILE : (b + 1) * TILE, :]
        sources_ref[(2 * tiles - 1 - b) * TILE : (2 * tiles - b) * TILE, :] = before[b * TILE : (b + 1) * TILE]
    width = taps_ref.shape[1]
    count = sources_ref.shape[0] // TILE
    further, _, chans = ahead_ref.shape
    masks = doc_masks(lengths_ref, [2 * m for m in range(1, further + 1)], chans)
    rounded = taps_ref[...].astype(BF16).astype(F32)
    skewed = pltpu.roll(jnp.broadcast_to(rounded, (TILE, width)), 0, 1, stride=1, stride_axis=0)
    flip = flip_matrix()
    for d in range(width // TILE):
        block = skewed[:, d * TILE : (d + 1) * TILE]
        if d == 0:
            row = lax.broadcasted_iota(jnp.int32, block.shape, 0)
            col = lax.broadcasted_iota(jnp.int32, block.shape, 1)
            block = jnp.where(col >= row, block, 0.0)
        block = block.astype(BF16)
        later_ref[:, d * TILE : (d + 1) * TILE] = block
        earlier_ref[:, d * TILE : (d + 1) * TILE] = lax.dot_general(
            block, flip, (((0,), (0,)), ((), ())), preferred_element_type=F32
        ).astype(BF16)
    for m in range(1, further + 1):
        for b in range(count // 2):
            first = m * count + b + 1 - count // 2
            part = jnp.dot(
                earlier_ref[:, first * TILE : (first + count) * TILE], sources_ref[...], preferred_element_type=F32
            )
            ahead_ref[m - 1, b * TILE : (b + 1) * TILE, :] = part.astype(BF16) * masks[m - 1]


def near_kernel(
    lengths_ref, value_ref, gate_in_ref, skip_ref, later_ref, earlier_ref, sources_ref, cots_ref,
    near_ref, grad_value_ref, grad_gate_ref, future_ref,
):
    longest, rows, chans = cots_ref.shape
    blocks = rows // TILE
    masks = doc_masks(lengths_ref, range(longest), chans)
    for k in range(longest):
        block = cots_ref[k] if k == 0 else cots_ref[k] * masks[k]
        future_ref[k * rows : (k + 1) * rows, :] = block
    skip = skip_ref[...]
    for b in range(blocks):
        here = slice(b * TILE, (b + 1) * TILE)
        transposed = jnp.dot(
            later_ref[:, : (longest * blocks - b) * TILE], future_ref[b * TILE :, :], preferred_element_type=F32
        )
        through = transposed + skip * cots_ref[0, here, :].astype(F32)
        gate_in, value = gate_in_ref[here, :].astype(F32), value_ref[here, :].astype(F32)
        grad_value_ref[here, :] = (through * gate_in).astype(BF16)
        grad_gate_ref[here, :] = (through * value).astype(BF16)
        newer = blocks - 1 - b
        convolved = jnp.dot(
            earlier_ref[:, : (2 * blocks - newer) * TILE], sources_ref[newer * TILE :, :], preferred_element_type=F32
        )
        near_ref[here, :] = convolved + skip * (gate_in * value).astype(BF16).astype(F32)


def sum_kernel(gathered_ref, picks_ref, layer_out_ref, total_ref, *, starts, scale):
    del layer_out_ref
    owned = total_ref.shape[1]
    total = jnp.sum(gathered_ref[:, 0, :], axis=0, keepdims=True)
    owner = total[:, : owned]
    for n, start in enumerate(starts):
        if start > 0:
            owner = jnp.where(picks_ref[n, 0:1, :owned] > 0.0, total[:, start : start + owned], owner)
    total_ref[...] = owner * scale


PARAMS = pltpu.CompilerParams(vmem_limit_bytes=LIMIT)
VMEM = pl.BlockSpec(memory_space=pltpu.VMEM)


def body(value_proj, gate_in, gate_out, skip_gain, filter_taps, doc_lengths, cotangent):
    rows, chans = value_proj.shape
    maxlag = filter_taps.shape[0]
    longest = maxlag // rows
    shards, groups = lax.axis_size("seq"), lax.axis_size("ch")
    block = jax.ShapeDtypeStruct((rows, chans), BF16)
    cot_gated = (cotangent.astype(F32) * gate_out.astype(F32)).astype(BF16)
    gated = (gate_in.astype(F32) * value_proj.astype(F32)).astype(BF16)
    flipped = gated.reshape(rows // TILE, TILE, chans)[:, ::-1].reshape(rows, chans)

    future = cot_gated[None]
    span = longest
    while span > 2:
        span //= 2
        future = jnp.concatenate([future, shifted(future, "seq", -span)], axis=0)
    before = rotated(flipped, "seq", 1)
    bits = max(future.shape[0].bit_length() - 1, 1)
    order = sorted(range(future.shape[0]), key=lambda n: int(format(n, f"0{bits}b")[::-1], 2))
    evens = future if len(order) <= 2 else jnp.stack([future[n] for n in order])
    odds = rotated(evens, "seq", -1)
    future = jnp.stack([evens, odds], axis=1).reshape(longest, rows, chans)

    owned = maxlag // shards
    starts = tuple(sorted({p * owned % TILE for p in range(shards)}))
    window = -(-(starts[-1] + owned) // TILE) * TILE
    lengths, skip, turned, masks, own, picks = pl.pallas_call(
        functools.partial(stage_kernel, owned=owned, starts=starts),
        out_shape=(
            jax.ShapeDtypeStruct((1, doc_lengths.shape[0]), jnp.int32),
            jax.ShapeDtypeStruct((1, chans), F32),
            jax.ShapeDtypeStruct((chans, rows), BF16),
            jax.ShapeDtypeStruct((evens.shape[0], 8, chans), F32),
            jax.ShapeDtypeStruct((TILE, rows), F32),
            jax.ShapeDtypeStruct((len(starts), 8, window), F32),
        ),
        in_specs=[VMEM] * 4,
        out_specs=(VMEM,) * 6,
        compiler_params=PARAMS,
        name="stage",
    )(doc_lengths.reshape(1, -1), skip_gain.reshape(1, chans), cot_gated, flipped)
    grad_scale = 1.0 / math.sqrt(shards * rows * chans * groups)
    parts = pl.pallas_call(
        functools.partial(lag_kernel, owned=owned, copies=groups, shards=shards),
        out_shape=jax.ShapeDtypeStruct((shards * groups, 1, window), F32),
        in_specs=[VMEM] * 7,
        out_specs=VMEM,
        compiler_params=PARAMS,
        cost_estimate=pl.CostEstimate(flops=LAGF, bytes_accessed=2**20, transcendentals=0),
        name="lags",
    )(masks, flipped, before, turned, own, evens, gate_out)
    gathered = lax.all_to_all(parts, ("ch", "seq"), 0, 0, tiled=True)

    band = jax.ShapeDtypeStruct((TILE, maxlag), BF16)
    further = longest // 2 - 1
    later, earlier, ahead, sources = pl.pallas_call(
        ahead_kernel,
        out_shape=(
            band, band, jax.ShapeDtypeStruct((further, rows, chans), BF16), jax.ShapeDtypeStruct((2 * rows, chans), BF16)
        ),
        in_specs=[VMEM] * 5 + [pl.BlockSpec(memory_space=pl.ANY)],
        out_specs=(VMEM,) * 4,
        compiler_params=PARAMS,
        name="ahead",
    )(lengths, filter_taps.reshape(1, maxlag), masks, flipped, before, parts)
    far = sum(shifted(ahead[m], "seq", 2 * m + 2).astype(F32) for m in range(further))

    near, grad_value, grad_gate = pl.pallas_call(
        near_kernel,
        out_shape=(jax.ShapeDtypeStruct((rows, chans), F32), block, block),
        in_specs=[VMEM] * 8,
        out_specs=(VMEM,) * 3,
        scratch_shapes=[pltpu.VMEM((maxlag, chans), BF16)],
        compiler_params=PARAMS,
        cost_estimate=pl.CostEstimate(flops=CONVF, bytes_accessed=2**20, transcendentals=0),
        name="near",
    )(lengths, value_proj, gate_in, skip, later, earlier, sources, future)
    layer_out = (gate_out.astype(F32) * (near + far)).astype(BF16)
    filter_grad = pl.pallas_call(
        functools.partial(sum_kernel, starts=starts, scale=grad_scale),
        out_shape=jax.ShapeDtypeStruct((1, owned), F32),
        in_specs=[VMEM, VMEM, pl.BlockSpec(memory_space=pl.ANY)],
        out_specs=VMEM,
        compiler_params=PARAMS,
        name="sum",
    )(gathered, picks, layer_out)[0]
    return (layer_out, grad_value, grad_gate, filter_grad)


def solution(mesh):
    placed = (P("seq", "ch"), P("seq", "ch"), P("seq", "ch"), P("ch"), P(), P(), P("seq", "ch"))
    return jax.shard_map(
        body,
        mesh=mesh,
        in_specs=placed,
        out_specs=(P("seq", "ch"), P("seq", "ch"), P("seq", "ch"), P("seq")),
        check_vma=False,
    )
```
